32 devices in a mesh: grp: 2 (over y), row: 4 (over z), col: 2 (over x), sub: 2 (over core).
Axes of the slice: x: 2, y: 2, z: 4, core: 2. Of those that a mesh axis runs over, the one named last changes fastest.
Arguments:
- a_blocks: bfloat16 [16, 2, 4, 2, 256, 256], P(('grp', 'row', 'sub'), 'col'), parts along dimension 0, may hold values from 20 to 2000
- block_list: int32 [16, 2, 4, 2], P(('grp', 'row', 'sub'), 'col'), parts along dimension 0, may hold values from 0 to 3, as said below
- block_count: int32 [16, 2, 4], P(('grp', 'row', 'sub'), 'col'), parts along dimension 0, may hold values from 1 to 2
- w_factor: bfloat16 [16, 1024, 256], P(('grp', 'row', 'sub')), parts along dimension 0, may hold values from 0.05 to 4
- h_factor: bfloat16 [256, 4096], P(None, ('grp', 'row', 'col')), parts along dimension 1, may hold values from 0.05 to 4
Outputs:
- w_new: float32 [16, 1024, 256], P(('grp', 'row', 'sub'), 'col'), parts along dimension 0
- h_new: float32 [256, 4096], P(None, ('grp', 'row', 'col')), parts along dimension 1
The draws below stay inside these ranges and needn't reach their ends.
There are 2 independent parts, one for each index of `grp`. The reference program is written for one: setup_inputs(seed, part) draws one part's arguments, and reference() takes and returns one part's arrays. A program takes and returns all parts, laid end to end along the dimension named above; each array names one. Nothing has to cross between parts.
Inputs may be any that keep to these rules, and one draw needn't show every extreme that they name: `block_list`: within one block row and column group the 2 slots name different column blocks.
All inputs are finite; a program needn't handle non-finite values.
Results may differ from the reference program's by a relative error of at most 0.0003.
Values may be sent and summed in bfloat16 or wider, within the bound.
A program may use at most 64 MiB of HBM per device.

```python
import math
import jax
import jax.numpy as jnp
from jax import lax

RANK = 256
BLOCK = 256
ROW_BLOCKS = 4
SLOTS = 2
TILES = 8
TILE_ROWS = 1024
COLUMNS = 2048
N_ROW = 4
N_COL = 2


def draw_block_list(key, part):
    total = TILES * N_COL * ROW_BLOCKS
    keys = jax.random.split(jax.random.fold_in(key, 11), total)
    chosen = jax.vmap(lambda k: jax.random.permutation(k, N_ROW)[:SLOTS])(keys)
    return chosen.reshape(TILES, N_COL, ROW_BLOCKS, SLOTS).astype(jnp.int32)


def draw_block_count(key, part):
    total = TILES * N_COL * ROW_BLOCKS
    first = jax.random.randint(jax.random.fold_in(key, 21), (total,), 1, SLOTS + 1)
    second = jax.random.randint(jax.random.fold_in(key, 22), (total,), 1, SLOTS + 1)
    counts = jnp.minimum(first, second)
    pick = jax.random.randint(jax.random.fold_in(key, 23), (), 0, total)
    counts = jnp.where(jnp.arange(total) == pick, SLOTS, counts)
    return counts.reshape(TILES, N_COL, ROW_BLOCKS).astype(jnp.int32)


def draw_w_factor(key, part):
    shape = (TILES, TILE_ROWS, RANK)
    position = jnp.arange(TILES, dtype=jnp.float32)[:, None, None] / max(TILES - 1, 1)
    base = jnp.exp(jax.random.uniform(jax.random.fold_in(key, 32), shape, jnp.float32, jnp.log(0.1), 0.0))
    factor = jnp.power(3.0, position)
    return (base * factor).astype(jnp.bfloat16)


def draw_h_factor(key, part):
    shape = (RANK, COLUMNS)
    blocks = N_ROW * N_COL
    position = (jnp.arange(COLUMNS, dtype=jnp.int32) // BLOCK).astype(jnp.float32)[None, :] / max(blocks - 1, 1)
    base = jnp.exp(jax.random.uniform(jax.random.fold_in(key, 42), shape, jnp.float32, jnp.log(0.1), 0.0))
    factor = jnp.power(3.0, position)
    return (base * factor).astype(jnp.bfloat16)


def block_scale(rng, shape, cuts, low, largest):
    factor_of = 1.0
    for dim, shards_of in cuts:
        draws = jax.random.uniform(jax.random.fold_in(jax.random.fold_in(rng, 6), dim), (shards_of,), jnp.float32, low / len(cuts), largest / len(cuts))
        factor_of = factor_of * jnp.repeat(jnp.exp(draws), shape[dim] // shards_of).reshape((-1,) + (1,) * (len(shape) - 1 - dim))
    return factor_of


def setup_inputs(seed: int = 0, part: int = 0) -> dict:
    key_list = jax.random.split(jax.random.key(seed), 6)
    part_keys = jax.random.split(jax.random.fold_in(key_list[5], part), 6)
    a_blocks = jnp.clip(jnp.exp(math.log(2000.0) - 4.6051702 * jax.random.uniform(part_keys[0], (TILES, N_COL, ROW_BLOCKS, SLOTS, BLOCK, BLOCK), jnp.float32) ** block_scale(part_keys[0], (TILES, N_COL, ROW_BLOCKS, SLOTS, BLOCK, BLOCK), ((0, 8), (1, 2)), -0.2, 0.2)), 20.0, 2000.0).astype(jnp.bfloat16)
    block_list = draw_block_list(jax.random.fold_in(jax.random.fold_in(key_list[5], part), 71), part)
    block_count = draw_block_count(jax.random.fold_in(jax.random.fold_in(key_list[5], part), 71), part)
    w_factor = draw_w_factor(jax.random.fold_in(jax.random.fold_in(key_list[5], part), 71), part)
    h_factor = draw_h_factor(jax.random.fold_in(jax.random.fold_in(key_list[5], part), 71), part)
    return dict(a_blocks=a_blocks, block_list=block_list, block_count=block_count, w_factor=w_factor, h_factor=h_factor)


def reference(a_blocks, block_list, block_count, w_factor, h_factor):
    w_total = jnp.sum(w_factor.astype(jnp.float32), axis=(0, 1))
    h_total = jnp.sum(h_factor.astype(jnp.float32), axis=1)
    total_slots = TILES * N_COL * ROW_BLOCKS * SLOTS
    numer_w = jnp.zeros((TILES, TILE_ROWS, RANK), jnp.float32)
    numer_h = jnp.zeros((RANK, COLUMNS), jnp.float32)

    def visit(state, index):
        slot_idx = index % SLOTS
        rest = index // SLOTS
        brow = rest % ROW_BLOCKS
        rest = rest // ROW_BLOCKS
        group = rest % N_COL
        tile = (rest // N_COL).astype(jnp.int32)
        matches = slot_idx < block_count[tile, group, brow]
        column = (block_list[tile, group, brow, slot_idx] * N_COL + group).astype(jnp.int32)
        row_start = (brow * BLOCK).astype(jnp.int32)
        col_start = (column * BLOCK).astype(jnp.int32)
        zero = jnp.int32(0)

        def compute(state):
            numer_w, numer_h = state
            w_rows = lax.dynamic_slice(w_factor, (tile, row_start, zero), (1, BLOCK, RANK))[0]
            h_block = lax.dynamic_slice(h_factor, (zero, col_start), (RANK, BLOCK))
            values = a_blocks[tile, group, brow, slot_idx]
            product = jnp.dot(w_rows, h_block, preferred_element_type=jnp.float32)
            ratios = (values.astype(jnp.float32) / product).astype(jnp.bfloat16)
            part_h = jnp.dot(w_rows.T, ratios, preferred_element_type=jnp.float32)
            part_w = jnp.dot(ratios, h_block.T, preferred_element_type=jnp.float32)
            old_h = lax.dynamic_slice(numer_h, (zero, col_start), (RANK, BLOCK))
            numer_h = lax.dynamic_update_slice(numer_h, old_h + part_h, (zero, col_start))
            old_w = lax.dynamic_slice(numer_w, (tile, row_start, zero), (1, BLOCK, RANK))
            numer_w = lax.dynamic_update_slice(numer_w, old_w + part_w[None], (tile, row_start, zero))
            return numer_w, numer_h

        return lax.cond(matches, compute, lambda st: st, state), None

    (numer_w, numer_h), _ = lax.scan(visit, (numer_w, numer_h), jnp.arange(total_slots, dtype=jnp.int32))
    w_new = w_factor.astype(jnp.float32) * numer_w / h_total[None, None, :]
    h_new = h_factor.astype(jnp.float32) * numer_h / w_total[:, None]
    return w_new, h_new
```

```python
import functools
import jax
import jax.numpy as jnp
from jax import lax
from jax.experimental import pallas as pl
from jax.experimental.pallas import tpu as pltpu
from jax.sharding import PartitionSpec as P

MESH = pl.DeviceIdType.MESH
UNROLL = 8


def when(condition, action):
    if isinstance(condition, bool):
        if condition:
            action()
    else:
        pl.when(condition)(action)


def each(count, action, first=0):
    if count <= UNROLL:
        for i in range(first, count):
            action(i)
    else:

        def step(i, carry):
            action(i)
            return carry

        lax.fori_loop(first, count, step, 0)


def kernel(
    sizes, a_hbm, lists, counts, w_hbm, h_hbm, w_out, h_out,
    a_v, w_v, wt_v, hall, ratios, nw, nh, nhx, nrecv, wrecv, hsum, hrecv, wsum, wsrecv,
    w_stage, h_stage, load_sem, out_sem,
    hs_sem, hr_sem, fs_sem, fr_sem, xs_sem, xr_sem, zs_sem, zr_sem,
    ws_sem, wr_sem, gs_sem, gr_sem, ts_sem, tr_sem, os_sem, or_sem,
):
    n_row, n_col, n_sub = sizes
    row, col, sub = lax.axis_index("row"), lax.axis_index("col"), lax.axis_index("sub")
    other = 1 - sub
    row_blocks, slots, width, _ = a_v.shape
    tile_rows, rank = w_v.shape
    half = rank // n_sub
    share = tile_rows // n_col
    mine = pl.ds(pl.multiple_of(sub * half, half), half)
    theirs = pl.ds(pl.multiple_of(other * half, half), half)

    def ahead(j):
        return lax.rem(row + j, n_row)

    def behind(j):
        return lax.rem(row + n_row - j, n_row)

    load_h = pltpu.make_async_copy(h_hbm, hall.at[row], load_sem.at[0])
    load_w = pltpu.make_async_copy(w_hbm, w_v, load_sem.at[1])
    load_a = pltpu.make_async_copy(a_hbm, a_v, load_sem.at[2])
    load_w.start()
    load_h.start()
    load_a.start()

    barrier = pltpu.get_barrier_semaphore()

    def greet(i):
        jr, js = i // n_sub, i % n_sub
        pl.semaphore_signal(
            barrier, inc=1, device_id={"row": ahead(jr), "sub": lax.rem(sub + js, n_sub)},
            device_id_type=MESH,
        )

    each(n_row * n_sub, greet, 1)

    def greet_col(j):
        pl.semaphore_signal(
            barrier, inc=1, device_id={"col": lax.rem(col + j, n_col)}, device_id_type=MESH
        )

    each(n_col, greet_col, 1)
    pl.semaphore_wait(barrier, n_row * n_sub - 1 + n_col - 1)

    def h_copy(j):
        return pltpu.make_async_remote_copy(
            src_ref=h_hbm.at[mine], dst_ref=hall.at[row, mine],
            send_sem=hs_sem.at[j], recv_sem=hr_sem.at[j],
            device_id={"row": ahead(j)}, device_id_type=MESH,
        )

    def h_arrival(j):
        return pltpu.make_async_remote_copy(
            src_ref=h_hbm.at[mine], dst_ref=hall.at[behind(j), mine],
            send_sem=hs_sem.at[j], recv_sem=hr_sem.at[j],
            device_id={"row": ahead(j)}, device_id_type=MESH,
        )

    def forward(j, part):
        return pltpu.make_async_remote_copy(
            src_ref=hall.at[behind(j), part], dst_ref=hall.at[behind(j), part],
            send_sem=fs_sem.at[j], recv_sem=fr_sem.at[j],
            device_id={"sub": other}, device_id_type=MESH,
        )

    def w_sum_copy(i):
        jr, js = i // n_sub, i % n_sub
        return pltpu.make_async_remote_copy(
            src_ref=wsum, dst_ref=wsrecv.at[i],
            send_sem=ts_sem.at[i], recv_sem=tr_sem.at[i],
            device_id={"row": ahead(jr), "sub": lax.rem(sub + js, n_sub)}, device_id_type=MESH,
        )

    def swap(j):
        return pltpu.make_async_remote_copy(
            src_ref=nh.at[j, theirs], dst_ref=nhx.at[j],
            send_sem=xs_sem.at[j], recv_sem=xr_sem.at[j],
            device_id={"sub": other}, device_id_type=MESH,
        )

    def h_numer_copy(j):
        return pltpu.make_async_remote_copy(
            src_ref=nhx.at[j], dst_ref=nrecv.at[j],
            send_sem=zs_sem.at[j], recv_sem=zr_sem.at[j],
            device_id={"row": behind(j)}, device_id_type=MESH,
        )

    def w_numer_copy(j):
        to = lax.rem(col + j, n_col)
        return pltpu.make_async_remote_copy(
            src_ref=nw.at[pl.ds(pl.multiple_of(to * share, share), share)], dst_ref=wrecv.at[j],
            send_sem=ws_sem.at[j], recv_sem=wr_sem.at[j],
            device_id={"col": to}, device_id_type=MESH,
        )

    def h_sum_copy(j):
        return pltpu.make_async_remote_copy(
            src_ref=hsum, dst_ref=hrecv.at[j],
            send_sem=gs_sem.at[j], recv_sem=gr_sem.at[j],
            device_id={"col": lax.rem(col + j, n_col)}, device_id_type=MESH,
        )

    if n_row <= UNROLL:
        order = [0]
        for j in range(1, n_row):
            order.append((j + 1) // 2 if j % 2 else n_row - j // 2)
    else:
        order = None

    def send_h(i):
        h_copy(i if order is None else order[i]).start()

    each(n_row, send_h, 1)

    load_w.wait()
    wsum[...] = jnp.dot(
        jnp.ones((8, tile_rows), jnp.bfloat16), w_v[...], preferred_element_type=jnp.float32
    )
    each(n_row * n_sub, lambda i: w_sum_copy(i).start(), 1)
    wt_v[...] = w_v[...].T
    load_h.wait()
    load_a.wait()

    def reduce_pair(j):
        swap(j).wait()
        nhx[j] = nhx[j] + nh[j, mine, :]

    def turn(i):
        j = i if order is None else order[i]
        before = i - 1 if order is None else order[i - 1]
        first = i == 0
        last = i == n_row - 1

        def receive():
            h_arrival(j).wait_recv()
            forward(j, mine).start()

        def pass_on():
            swap(before).wait()
            nhx[before] = nhx[before] + nh[before, mine, :]

            def send():
                h_numer_copy(before).start()

            when(i > 1, send)

        when(i > 0, receive)
        when(i > 0, pass_on)
        when(i > 0, lambda: forward(j, theirs).wait_recv())
        target = behind(j)
        h_block = hall[target]
        part = lax.dot_general(
            jnp.ones((8, width), jnp.bfloat16), h_block, (((1,), (1,)), ((), ())),
            preferred_element_type=jnp.float32,
        )
        for brow in range(row_blocks):
            rows = pl.ds(brow * width, width)
            position = jnp.int32(0)
            live = jnp.float32(0)
            for slot in range(slots):
                match = (lists[brow, slot] == target) & (slot < counts[brow])
                position = jnp.where(match, slot, position)
                live = jnp.where(match, jnp.float32(1), live)
            product = jnp.dot(w_v[rows, :], h_block, preferred_element_type=jnp.float32)
            entries = a_v[brow, position].astype(jnp.float32) * live
            ratio = (entries / product).astype(jnp.bfloat16)
            ratios[rows, :] = ratio
            part_w = lax.dot_general(
                ratio, h_block, (((1,), (1,)), ((), ())), preferred_element_type=jnp.float32
            )
            if order is None:
                nw[rows, :] = jnp.where(first, 0.0, nw[rows, :]) + part_w
            elif first:
                nw[rows, :] = part_w
            else:
                nw[rows, :] = nw[rows, :] + part_w
        if order is None:
            hsum[...] = jnp.where(first, 0.0, hsum[...]) + part
        elif first:
            hsum[...] = part
        else:
            hsum[...] = hsum[...] + part

        def send_w():
            each(n_col, lambda k: w_numer_copy(k).start(), 1)
            each(n_col, lambda k: h_sum_copy(k).start(), 1)

        when(last, send_w)
        nh[j] = jnp.dot(wt_v[...], ratios[...], preferred_element_type=jnp.float32)
        swap(j).start()

    if order is None:
        nw[...] = jnp.zeros_like(nw)
        hsum[...] = jnp.zeros_like(hsum)
    each(n_row, turn)
    final = n_row - 1 if order is None else order[-1]
    swap(final).wait()
    nhx[final] = nhx[final] + nh[final, mine, :]
    h_numer_copy(final).start()

    def add_w_sum(i):
        w_sum_copy(i).wait()
        wsrecv[0] = wsrecv[0] + wsrecv[i]

    wsrecv[0] = wsum[...]
    each(n_row * n_sub, add_w_sum, 1)
    down = lax.broadcasted_iota(jnp.int32, (half, rank), 0) + sub * half
    along = lax.broadcasted_iota(jnp.int32, (half, rank), 1)
    w_total = jnp.sum(
        jnp.where(down == along, wsrecv[0, 0:1, :], 0.0), axis=1, keepdims=True
    )

    def add_h_numer(j):
        h_numer_copy(j).wait()
        nhx[0] = nhx[0] + nrecv[j]

    each(n_row, add_h_numer, 1)
    h_stage[...] = hall[row, mine, :].astype(jnp.float32) * nhx[0] / w_total
    h_finish = pltpu.make_async_remote_copy(
        src_ref=h_stage, dst_ref=h_out.at[mine], send_sem=os_sem, recv_sem=or_sem,
        device_id={"sub": other}, device_id_type=MESH,
    )
    h_finish.start()
    h_local = pltpu.make_async_copy(h_stage, h_out.at[mine], out_sem.at[0])
    h_local.start()

    def add_h_sum(j):
        h_sum_copy(j).wait()

    each(n_col, add_h_sum, 1)
    h_total = hsum[0:1, :]
    for j in range(1, n_col):
        h_total = h_total + hrecv[j, 0:1, :]
    own = pl.ds(pl.multiple_of(col * share, share), share)
    each(n_col, lambda j: w_numer_copy(j).wait(), 1)
    total = nw[own, :]
    for j in range(1, n_col):
        total = total + wrecv[j]
    w_stage[...] = w_v[own, :].astype(jnp.float32) * total / h_total
    w_local = pltpu.make_async_copy(w_stage, w_out, out_sem.at[1])
    w_local.start()

    def settle(j):
        h_copy(j).wait_send()
        forward(j, mine).wait_send()

    each(n_row, settle, 1)
    h_finish.wait()
    h_local.wait()
    w_local.wait()


def body(a_blocks, block_list, block_count, w_factor, h_factor):
    n_row, n_col, n_sub = (lax.axis_size(axis) for axis in ("row", "col", "sub"))
    a, lists, counts, w = a_blocks[0, 0], block_list[0, 0], block_count[0, 0], w_factor[0]
    tile_rows, rank = w.shape
    width = h_factor.shape[1]
    half = rank // n_sub
    share = tile_rows // n_col
    f32, bf16 = jnp.float32, jnp.bfloat16
    dma = pltpu.SemaphoreType.DMA
    vmem, smem = pltpu.VMEM, pltpu.SMEM
    anywhere = pl.BlockSpec(memory_space=pl.ANY)
    scalars = pl.BlockSpec(memory_space=smem)
    w_new, h_new = pl.pallas_call(
        functools.partial(kernel, (n_row, n_col, n_sub)),
        out_shape=(
            jax.ShapeDtypeStruct((share, rank), f32),
            jax.ShapeDtypeStruct((rank, width), f32),
        ),
        in_specs=[anywhere, scalars, scalars, anywhere, anywhere],
        out_specs=(anywhere, anywhere),
        scratch_shapes=[
            vmem(a.shape, bf16),
            vmem(w.shape, bf16),
            vmem((rank, tile_rows), bf16),
            vmem((n_row, rank, width), bf16),
            vmem((tile_rows, width), bf16),
            vmem((tile_rows, rank), f32),
            vmem((n_row, rank, width), f32),
            vmem((n_row, half, width), f32),
            vmem((n_row, half, width), f32),
            vmem((n_col, share, rank), f32),
            vmem((8, rank), f32),
            vmem((n_col, 8, rank), f32),
            vmem((8, rank), f32),
            vmem((n_row * n_sub, 8, rank), f32),
            vmem((share, rank), f32),
            vmem((half, width), f32),
            dma((3,)),
            dma((2,)),
            *[dma((n_row,))] * 8,
            *[dma((n_col,))] * 4,
            *[dma((n_row * n_sub,))] * 2,
            dma,
            dma,
        ],
        compiler_params=pltpu.CompilerParams(
            collective_id=0, has_side_effects=True, vmem_limit_bytes=48 * 2**20
        ),
    )(a, lists, counts, w, h_factor)
    return w_new[None], h_new


def solution(mesh):
    placed = (
        P(("grp", "row", "sub"), "col", None, None, None, None),
        P(("grp", "row", "sub"), "col", None, None),
        P(("grp", "row", "sub"), "col", None),
        P(("grp", "row", "sub"), None, None),
        P(None, ("grp", "row", "col")),
    )
    return jax.shard_map(
        body,
        mesh=mesh,
        in_specs=placed,
        out_specs=(P(("grp", "row", "sub"), "col", None), P(None, ("grp", "row", "col"))),
        check_vma=False,
    )
```

```python
import functools
import jax
import jax.numpy as jnp
from jax import lax
from jax.experimental import pallas as pl
from jax.experimental.pallas import tpu as pltpu
from jax.sharding import PartitionSpec as P

MESH = pl.DeviceIdType.MESH
UNROLL = 8
LEVELS = 65535.0
OFFSET = 32768


def when(condition, action):
    if isinstance(condition, bool):
        if condition:
            action()
    else:
        pl.when(condition)(action)


def each(count, action, first=0):
    if count <= UNROLL:
        for i in range(first, count):
            action(i)
    else:

        def step(i, carry):
            action(i)
            return carry

        lax.fori_loop(first, count, step, 0)


def encode(values, code, scale):
    top = jnp.maximum(jnp.max(values, axis=0, keepdims=True), 1e-30)
    steps = (values * (LEVELS / top) + 0.5).astype(jnp.int32) - OFFSET
    code[...] = steps.astype(jnp.int16)
    scale[...] = jnp.broadcast_to(top * (1.0 / LEVELS), scale.shape)


def decode(code, scale):
    return (code.astype(jnp.int32) + OFFSET).astype(jnp.float32) * scale[0:1, :]


def kernel(
    sizes, a_hbm, lists_hbm, counts_hbm, w_hbm, h_hbm, w_out, h_out,
    lists, counts, a_v, w_v, wt_v, hall, ratios, nw, nh, nhx,
    hq, hq_scale, hq_in, hq_scale_in, wq, wq_scale, wq_in, wq_scale_in,
    hsum, hrecv, wsum, wsrecv, w_inverse, load_sem,
    hs_sem, hr_sem, fs_sem, fr_sem, xs_sem, xr_sem, zs_sem, zr_sem, ys_sem, yr_sem,
    ws_sem, wr_sem, vs_sem, vr_sem, gs_sem, gr_sem, ts_sem, tr_sem, os_sem, or_sem,
):
    n_row, n_col, n_sub = sizes
    row, col, sub = lax.axis_index("row"), lax.axis_index("col"), lax.axis_index("sub")
    other = 1 - sub
    row_blocks, slots, width, _ = a_v.shape
    tile_rows, rank = w_v.shape
    half = rank // n_sub
    share = tile_rows // n_col
    per_share = share // width
    away = row_blocks - per_share
    mine = pl.ds(pl.multiple_of(sub * half, half), half)
    theirs = pl.ds(pl.multiple_of(other * half, half), half)

    def ahead(j):
        return lax.rem(row + j, n_row)

    def behind(j):
        return lax.rem(row + n_row - j, n_row)

    load_h = pltpu.make_async_copy(h_hbm, hall.at[row], load_sem.at[0])
    load_w = pltpu.make_async_copy(w_hbm, w_v, load_sem.at[1])
    load_a = pltpu.make_async_copy(a_hbm, a_v, load_sem.at[2])
    load_lists = pltpu.make_async_copy(lists_hbm, lists, load_sem.at[3])
    load_counts = pltpu.make_async_copy(counts_hbm, counts, load_sem.at[4])
    load_w.start()
    load_h.start()
    load_lists.start()
    load_counts.start()
    load_a.start()

    barrier = pltpu.get_barrier_semaphore()

    def greet(i):
        jr, js = i // n_sub, i % n_sub
        pl.semaphore_signal(
            barrier, inc=1, device_id={"row": ahead(jr), "sub": lax.rem(sub + js, n_sub)},
            device_id_type=MESH,
        )

    each(n_row * n_sub, greet, 1)

    def greet_col(j):
        pl.semaphore_signal(
            barrier, inc=1, device_id={"col": lax.rem(col + j, n_col)}, device_id_type=MESH
        )

    each(n_col, greet_col, 1)
    pl.semaphore_wait(barrier, n_row * n_sub - 1 + n_col - 1)

    def h_copy(j):
        return pltpu.make_async_remote_copy(
            src_ref=h_hbm.at[mine], dst_ref=hall.at[row, mine],
            send_sem=hs_sem.at[j], recv_sem=hr_sem.at[j],
            device_id={"row": ahead(j)}, device_id_type=MESH,
        )

    def h_arrival(j):
        return pltpu.make_async_remote_copy(
            src_ref=h_hbm.at[mine], dst_ref=hall.at[behind(j), mine],
            send_sem=hs_sem.at[j], recv_sem=hr_sem.at[j],
            device_id={"row": ahead(j)}, device_id_type=MESH,
        )

    def forward(j, part):
        return pltpu.make_async_remote_copy(
            src_ref=hall.at[behind(j), part], dst_ref=hall.at[behind(j), part],
            send_sem=fs_sem.at[j], recv_sem=fr_sem.at[j],
            device_id={"sub": other}, device_id_type=MESH,
        )

    def w_sum_copy(i):
        jr, js = i // n_sub, i % n_sub
        return pltpu.make_async_remote_copy(
            src_ref=wsum, dst_ref=wsrecv.at[i],
            send_sem=ts_sem.at[i], recv_sem=tr_sem.at[i],
            device_id={"row": ahead(jr), "sub": lax.rem(sub + js, n_sub)}, device_id_type=MESH,
        )

    def swap(j):
        return pltpu.make_async_remote_copy(
            src_ref=nh.at[j, theirs], dst_ref=nhx.at[j],
            send_sem=xs_sem.at[j], recv_sem=xr_sem.at[j],
            device_id={"sub": other}, device_id_type=MESH,
        )

    def h_numer_copy(j):
        return pltpu.make_async_remote_copy(
            src_ref=hq.at[j], dst_ref=hq_in.at[j],
            send_sem=zs_sem.at[j], recv_sem=zr_sem.at[j],
            device_id={"row": behind(j)}, device_id_type=MESH,
        )

    def h_scale_copy(j):
        return pltpu.make_async_remote_copy(
            src_ref=hq_scale.at[j], dst_ref=hq_scale_in.at[j],
            send_sem=ys_sem.at[j], recv_sem=yr_sem.at[j],
            device_id={"row": behind(j)}, device_id_type=MESH,
        )

    def w_numer_copy(i):
        return pltpu.make_async_remote_copy(
            src_ref=wq.at[i], dst_ref=wq_in.at[i],
            send_sem=ws_sem.at[i], recv_sem=wr_sem.at[i],
            device_id={"col": lax.rem(col + 1 + i // per_share, n_col)}, device_id_type=MESH,
        )

    def w_scale_copy(i):
        return pltpu.make_async_remote_copy(
            src_ref=wq_scale.at[i], dst_ref=wq_scale_in.at[i],
            send_sem=vs_sem.at[i], recv_sem=vr_sem.at[i],
            device_id={"col": lax.rem(col + 1 + i // per_share, n_col)}, device_id_type=MESH,
        )

    def h_sum_copy(j):
        return pltpu.make_async_remote_copy(
            src_ref=hsum, dst_ref=hrecv.at[j],
            send_sem=gs_sem.at[j], recv_sem=gr_sem.at[j],
            device_id={"col": lax.rem(col + j, n_col)}, device_id_type=MESH,
        )

    if n_row <= UNROLL:
        order = [0]
        for j in range(1, n_row):
            order.append((j + 1) // 2 if j % 2 else n_row - j // 2)
    else:
        order = None

    def send_h(i):
        h_copy(i if order is None else order[i]).start()

    each(n_row, send_h, 1)

    load_w.wait()
    wsum[...] = jnp.dot(
        jnp.ones((8, tile_rows), jnp.bfloat16), w_v[...], preferred_element_type=jnp.float32
    )
    each(n_row * n_sub, lambda i: w_sum_copy(i).start(), 1)
    wt_v[...] = w_v[...].T
    load_h.wait()
    load_a.wait()

    load_lists.wait()
    load_counts.wait()

    def add_w_sums():
        def add(i):
            w_sum_copy(i).wait()
            wsrecv[0] = wsrecv[0] + wsrecv[i]

        wsrecv[0] = wsum[...]
        each(n_row * n_sub, add, 1)
        down = lax.broadcasted_iota(jnp.int32, (half, rank), 0) + sub * half
        along = lax.broadcasted_iota(jnp.int32, (half, rank), 1)
        total = jnp.sum(
            jnp.where(down == along, wsrecv[0, 0:1, :], 0.0), axis=1, keepdims=True
        )
        w_inverse[...] = jnp.broadcast_to(1.0 / total, (half, width))

    def add_pair(j):
        swap(j).wait()
        numer = nhx[j] + nh[j, mine, :]
        return hall[behind(j), mine, :].astype(jnp.float32) * numer * w_inverse[...]

    def send_numer(j):
        encode(add_pair(j), hq.at[j], hq_scale.at[j])
        h_numer_copy(j).start()
        h_scale_copy(j).start()

    def turn(i):
        j = i if order is None else order[i]
        before = i - 1 if order is None else order[i - 1]
        first = i == 0
        last = i == n_row - 1

        def receive():
            h_arrival(j).wait_recv()
            forward(j, mine).start()

        def add_own():
            add_w_sums()
            h_out[mine, :] = add_pair(before)

        when(i > 0, receive)
        when(i == 1, add_own)
        when(i > 1, lambda: send_numer(before))
        when(i > 0, lambda: forward(j, theirs).wait_recv())
        target = behind(j)
        h_block = hall[target]
        part = lax.dot_general(
            jnp.ones((8, width), jnp.bfloat16), h_block, (((1,), (1,)), ((), ())),
            preferred_element_type=jnp.float32,
        )
        for place in range(row_blocks):
            brow = lax.rem((col + 1) * per_share + place, row_blocks)
            rows = pl.ds(pl.multiple_of(brow * width, width), width)
            position = jnp.int32(0)
            live = jnp.float32(0)
            for slot in range(slots):
                match = (lists[slot, brow] == target) & (slot < counts[brow])
                position = jnp.where(match, slot, position)
                live = jnp.where(match, jnp.float32(1), live)
            product = jnp.dot(w_v[rows, :], h_block, preferred_element_type=jnp.float32)
            entries = a_v[brow, position].astype(jnp.float32) * live
            ratio = (entries / product).astype(jnp.bfloat16)
            ratios[rows, :] = ratio
            part_w = lax.dot_general(
                ratio, h_block, (((1,), (1,)), ((), ())), preferred_element_type=jnp.float32
            )
            if order is None:
                nw[rows, :] = jnp.where(first, 0.0, nw[rows, :]) + part_w
            elif first:
                nw[rows, :] = part_w
            else:
                nw[rows, :] = nw[rows, :] + part_w

            def send_w(place=place, rows=rows):
                numer = w_v[rows, :].astype(jnp.float32) * nw[rows, :]
                encode(numer, wq.at[place], wq_scale.at[place])
                w_numer_copy(place).start()
                w_scale_copy(place).start()

            if place < away:
                when(last, send_w)
        if order is None:
            hsum[...] = jnp.where(first, 0.0, hsum[...]) + part
        elif first:
            hsum[...] = part
        else:
            hsum[...] = hsum[...] + part

        when(last, lambda: each(n_col, lambda k: h_sum_copy(k).start(), 1))
        nh[j] = jnp.dot(wt_v[...], ratios[...], preferred_element_type=jnp.float32)
        swap(j).start()

    if order is None:
        nw[...] = jnp.zeros_like(nw)
        hsum[...] = jnp.zeros_like(hsum)
    each(n_row, turn)
    final = n_row - 1 if order is None else order[-1]
    send_numer(final)

    each(n_col, lambda j: h_sum_copy(j).wait(), 1)
    h_total = hsum[0:1, :]
    for j in range(1, n_col):
        h_total = h_total + hrecv[j, 0:1, :]
    own = pl.ds(pl.multiple_of(col * share, share), share)
    w_out[...] = w_v[own, :].astype(jnp.float32) * nw[own, :]
    for i in range(away):
        rows = pl.ds(i % per_share * width, width)
        w_numer_copy(i).wait()
        w_scale_copy(i).wait()
        total = w_out[rows, :] + decode(wq_in[i], wq_scale_in[i])
        w_out[rows, :] = total / h_total if i >= away - per_share else total

    def add_h_numer(j):
        h_numer_copy(j).wait()
        h_scale_copy(j).wait()
        h_out[mine, :] = h_out[mine, :] + decode(hq_in[j], hq_scale_in[j])

    each(n_row, add_h_numer, 1)
    h_finish = pltpu.make_async_remote_copy(
        src_ref=h_out.at[mine], dst_ref=h_out.at[mine], send_sem=os_sem, recv_sem=or_sem,
        device_id={"sub": other}, device_id_type=MESH,
    )
    h_finish.start()

    def settle(j):
        h_copy(j).wait_send()
        forward(j, mine).wait_send()

    each(n_row, settle, 1)
    h_finish.wait_send()
    h_arrived = pltpu.make_async_remote_copy(
        src_ref=h_out.at[mine], dst_ref=h_out.at[theirs], send_sem=os_sem, recv_sem=or_sem,
        device_id={"sub": other}, device_id_type=MESH,
    )
    h_arrived.wait_recv()


def body(a_blocks, block_list, block_count, w_factor, h_factor):
    n_row, n_col, n_sub = (lax.axis_size(axis) for axis in ("row", "col", "sub"))
    a, lists, counts, w = a_blocks[0, 0], block_list[0, 0], block_count[0, 0], w_factor[0]
    tile_rows, rank = w.shape
    width = h_factor.shape[1]
    half = rank // n_sub
    share = tile_rows // n_col
    away = (tile_rows - share) // width
    f32, bf16, i16, i32 = jnp.float32, jnp.bfloat16, jnp.int16, jnp.int32
    dma = pltpu.SemaphoreType.DMA
    vmem, smem = pltpu.VMEM, pltpu.SMEM
    lists = lists.T
    w_new, h_new = pl.pallas_call(
        functools.partial(kernel, (n_row, n_col, n_sub)),
        out_shape=(
            jax.ShapeDtypeStruct((share, rank), f32),
            jax.ShapeDtypeStruct((rank, width), f32),
        ),
        in_specs=[pl.BlockSpec(memory_space=pltpu.HBM)] * 5,
        out_specs=(pl.BlockSpec(memory_space=vmem), pl.BlockSpec(memory_space=vmem)),
        scratch_shapes=[
            smem(lists.shape, i32),
            smem(counts.shape, i32),
            vmem(a.shape, bf16),
            vmem(w.shape, bf16),
            vmem((rank, tile_rows), bf16),
            vmem((n_row, rank, width), bf16),
            vmem((tile_rows, width), bf16),
            vmem((tile_rows, rank), f32),
            vmem((n_row, rank, width), f32),
            vmem((n_row, half, width), f32),
            vmem((n_row, half, width), i16),
            vmem((n_row, 8, width), f32),
            vmem((n_row, half, width), i16),
            vmem((n_row, 8, width), f32),
            vmem((away, width, rank), i16),
            vmem((away, 8, rank), f32),
            vmem((away, width, rank), i16),
            vmem((away, 8, rank), f32),
            vmem((8, rank), f32),
            vmem((n_col, 8, rank), f32),
            vmem((8, rank), f32),
            vmem((n_row * n_sub, 8, rank), f32),
            vmem((half, width), f32),
            dma((5,)),
            *[dma((n_row,))] * 10,
            *[dma((away,))] * 4,
            *[dma((n_col,))] * 2,
            *[dma((n_row * n_sub,))] * 2,
            dma,
            dma,
        ],
        compiler_params=pltpu.CompilerParams(
            collective_id=0, has_side_effects=True, vmem_limit_bytes=63 * 2**20
        ),
    )(a, lists, counts, w, h_factor)
    return w_new[None], h_new


def solution(mesh):
    placed = (
        P(("grp", "row", "sub"), "col", None, None, None, None),
        P(("grp", "row", "sub"), "col", None, None),
        P(("grp", "row", "sub"), "col", None),
        P(("grp", "row", "sub"), None, None),
        P(None, ("grp", "row", "col")),
    )
    return jax.shard_map(
        body,
        mesh=mesh,
        in_specs=placed,
        out_specs=(P(("grp", "row", "sub"), "col", None), P(None, ("grp", "row", "col"))),
        check_vma=False,
    )
```

```python
import functools
import jax
import jax.numpy as jnp
from jax import lax
from jax.experimental import pallas as pl
from jax.experimental.pallas import tpu as pltpu
from jax.sharding import PartitionSpec as P

MESH = pl.DeviceIdType.MESH
UNROLL = 8
LEVELS = 65535.0
OFFSET = 32768


def when(condition, action):
    if isinstance(condition, bool):
        if condition:
            action()
    else:
        pl.when(condition)(action)


def each(count, action, first=0):
    if count <= UNROLL:
        for i in range(first, count):
            action(i)
    else:

        def step(i, carry):
            action(i)
            return carry

        lax.fori_loop(first, count, step, 0)


def encode(values, code, scale):
    top = jnp.maximum(jnp.max(values, axis=0, keepdims=True), 1e-30)
    steps = (values * (LEVELS / top) + 0.5).astype(jnp.int32) - OFFSET
    code[...] = steps.astype(jnp.int16)
    scale[...] = jnp.broadcast_to(top * (1.0 / LEVELS), scale.shape)


def decode(code, scale):
    return (code.astype(jnp.int32) + OFFSET).astype(jnp.float32) * scale[0:1, :]


def kernel(
    sizes, a_hbm, lists_hbm, counts_hbm, w_hbm, h_hbm, w_out, h_out,
    lists, counts, a_v, w_v, wt_v, hall, ratios, nw, nh, nhx,
    hq, hq_scale, hq_in, hq_scale_in, wq, wq_scale, wq_in, wq_scale_in,
    hsum, hrecv, wsum, wsrecv, w_inverse, load_sem,
    hs_sem, hr_sem, fs_sem, fr_sem, xs_sem, xr_sem, zs_sem, zr_sem, ys_sem, yr_sem,
    ws_sem, wr_sem, vs_sem, vr_sem, gs_sem, gr_sem, ts_sem, tr_sem, os_sem, or_sem,
):
    n_row, n_col, n_sub = sizes
    row, col, sub = lax.axis_index("row"), lax.axis_index("col"), lax.axis_index("sub")
    other = 1 - sub
    row_blocks, slots, width, _ = a_v.shape
    tile_rows, rank = w_v.shape
    half = rank // n_sub
    share = tile_rows // n_col
    per_share = share // width
    away = row_blocks - per_share
    mine = pl.ds(pl.multiple_of(sub * half, half), half)
    theirs = pl.ds(pl.multiple_of(other * half, half), half)

    def ahead(j):
        return lax.rem(row + j, n_row)

    near = jnp.minimum(row, n_row - 1 - row)
    away_side = jnp.where(2 * row < n_row, 1, -1)

    def target(i):
        step = (i + 1) // 2
        sign = 1 - 2 * (i % 2)
        return row + jnp.where(i <= 2 * near, sign * step, away_side * (i - near))

    load_h = pltpu.make_async_copy(h_hbm, hall.at[row], load_sem.at[0])
    load_w = pltpu.make_async_copy(w_hbm, w_v, load_sem.at[1])
    load_a = pltpu.make_async_copy(a_hbm, a_v, load_sem.at[2])
    load_lists = pltpu.make_async_copy(lists_hbm, lists, load_sem.at[3])
    load_counts = pltpu.make_async_copy(counts_hbm, counts, load_sem.at[4])
    load_w.start()
    load_h.start()
    load_lists.start()
    load_counts.start()
    load_a.start()

    barrier = pltpu.get_barrier_semaphore()

    def greet(i):
        jr, js = i // n_sub, i % n_sub
        pl.semaphore_signal(
            barrier, inc=1, device_id={"row": ahead(jr), "sub": lax.rem(sub + js, n_sub)},
            device_id_type=MESH,
        )

    each(n_row * n_sub, greet, 1)

    def greet_col(j):
        pl.semaphore_signal(
            barrier, inc=1, device_id={"col": lax.rem(col + j, n_col)}, device_id_type=MESH
        )

    each(n_col, greet_col, 1)
    pl.semaphore_wait(barrier, n_row * n_sub - 1 + n_col - 1)

    def h_copy(i):
        return pltpu.make_async_remote_copy(
            src_ref=h_hbm.at[mine], dst_ref=hall.at[row, mine],
            send_sem=hs_sem.at[i], recv_sem=hr_sem.at[row],
            device_id={"row": target(i)}, device_id_type=MESH,
        )

    def h_arrival(i):
        return pltpu.make_async_remote_copy(
            src_ref=h_hbm.at[mine], dst_ref=hall.at[target(i), mine],
            send_sem=hs_sem.at[i], recv_sem=hr_sem.at[target(i)],
            device_id={"row": target(i)}, device_id_type=MESH,
        )

    def forward(i, part):
        return pltpu.make_async_remote_copy(
            src_ref=hall.at[target(i), part], dst_ref=hall.at[target(i), part],
            send_sem=fs_sem.at[i], recv_sem=fr_sem.at[i],
            device_id={"sub": other}, device_id_type=MESH,
        )

    def w_sum_copy(i):
        jr, js = i // n_sub, i % n_sub
        return pltpu.make_async_remote_copy(
            src_ref=wsum, dst_ref=wsrecv.at[i],
            send_sem=ts_sem.at[i], recv_sem=tr_sem.at[i],
            device_id={"row": ahead(jr), "sub": lax.rem(sub + js, n_sub)}, device_id_type=MESH,
        )

    def swap(j):
        return pltpu.make_async_remote_copy(
            src_ref=nh.at[j, theirs], dst_ref=nhx.at[j],
            send_sem=xs_sem.at[j], recv_sem=xr_sem.at[j],
            device_id={"sub": other}, device_id_type=MESH,
        )

    def h_numer_copy(i):
        return pltpu.make_async_remote_copy(
            src_ref=hq.at[i], dst_ref=hq_in.at[row],
            send_sem=zs_sem.at[i], recv_sem=zr_sem.at[row],
            device_id={"row": target(i)}, device_id_type=MESH,
        )

    def h_scale_copy(i):
        return pltpu.make_async_remote_copy(
            src_ref=hq_scale.at[i], dst_ref=hq_scale_in.at[row],
            send_sem=ys_sem.at[i], recv_sem=yr_sem.at[row],
            device_id={"row": target(i)}, device_id_type=MESH,
        )

    def h_numer_arrival(i):
        return pltpu.make_async_remote_copy(
            src_ref=hq.at[i], dst_ref=hq_in.at[target(i)],
            send_sem=zs_sem.at[i], recv_sem=zr_sem.at[target(i)],
            device_id={"row": target(i)}, device_id_type=MESH,
        )

    def h_scale_arrival(i):
        return pltpu.make_async_remote_copy(
            src_ref=hq_scale.at[i], dst_ref=hq_scale_in.at[target(i)],
            send_sem=ys_sem.at[i], recv_sem=yr_sem.at[target(i)],
            device_id={"row": target(i)}, device_id_type=MESH,
        )

    def w_numer_copy(i):
        return pltpu.make_async_remote_copy(
            src_ref=wq.at[i], dst_ref=wq_in.at[i],
            send_sem=ws_sem.at[i], recv_sem=wr_sem.at[i],
            device_id={"col": lax.rem(col + 1 + i // per_share, n_col)}, device_id_type=MESH,
        )

    def w_scale_copy(i):
        return pltpu.make_async_remote_copy(
            src_ref=wq_scale.at[i], dst_ref=wq_scale_in.at[i],
            send_sem=vs_sem.at[i], recv_sem=vr_sem.at[i],
            device_id={"col": lax.rem(col + 1 + i // per_share, n_col)}, device_id_type=MESH,
        )

    def h_sum_copy(j):
        return pltpu.make_async_remote_copy(
            src_ref=hsum, dst_ref=hrecv.at[j],
            send_sem=gs_sem.at[j], recv_sem=gr_sem.at[j],
            device_id={"col": lax.rem(col + j, n_col)}, device_id_type=MESH,
        )

    each(n_row, lambda i: h_copy(i).start(), 1)

    load_w.wait()
    wsum[...] = jnp.dot(
        jnp.ones((8, tile_rows), jnp.bfloat16), w_v[...], preferred_element_type=jnp.float32
    )
    each(n_row * n_sub, lambda i: w_sum_copy(i).start(), 1)
    wt_v[...] = w_v[...].T
    load_h.wait()
    load_a.wait()

    load_lists.wait()
    load_counts.wait()

    def add_w_sums():
        def add(i):
            w_sum_copy(i).wait()
            wsrecv[0] = wsrecv[0] + wsrecv[i]

        wsrecv[0] = wsum[...]
        each(n_row * n_sub, add, 1)
        down = lax.broadcasted_iota(jnp.int32, (half, rank), 0) + sub * half
        along = lax.broadcasted_iota(jnp.int32, (half, rank), 1)
        total = jnp.sum(
            jnp.where(down == along, wsrecv[0, 0:1, :], 0.0), axis=1, keepdims=True
        )
        w_inverse[...] = jnp.broadcast_to(1.0 / total, (half, width))

    def add_pair(j):
        swap(j).wait()
        numer = nhx[j] + nh[j, mine, :]
        return hall[target(j), mine, :].astype(jnp.float32) * numer * w_inverse[...]

    def send_numer(j):
        encode(add_pair(j), hq.at[j], hq_scale.at[j])
        h_numer_copy(j).start()
        h_scale_copy(j).start()

    def receive(i):
        h_arrival(i).wait_recv()
        forward(i, mine).start()

    def turn(i):
        first = i == 0
        last = i == n_row - 1
        when(i > 0, lambda: forward(i, theirs).wait_recv())
        block = target(i)
        h_block = hall[block]
        product = jnp.dot(w_v[...], h_block, preferred_element_type=jnp.float32)
        for brow in range(row_blocks):
            position = jnp.int32(0)
            live = jnp.float32(0)
            for slot in range(slots):
                match = (lists[slot, brow] == block) & (slot < counts[brow])
                position = jnp.where(match, slot, position)
                live = jnp.where(match, jnp.float32(1), live)
            rows = slice(brow * width, (brow + 1) * width)
            entries = a_v[brow, position].astype(jnp.float32) * live
            ratios[rows, :] = (entries / product[rows]).astype(jnp.bfloat16)
        if isinstance(i, int):
            when(0 < i < n_row - 1, lambda: receive(i + 1))
        else:
            when((0 < i) & (i < n_row - 1), lambda: receive(i + 1))
        part_w = lax.dot_general(
            ratios[...], h_block, (((1,), (1,)), ((), ())), preferred_element_type=jnp.float32
        )
        part_h = lax.dot_general(
            jnp.ones((8, width), jnp.bfloat16), h_block, (((1,), (1,)), ((), ())),
            preferred_element_type=jnp.float32,
        )
        if isinstance(i, int) and first:
            nw[...] = part_w
            hsum[...] = part_h
        else:
            nw[...] = nw[...] + part_w
            hsum[...] = hsum[...] + part_h

        def send_w():
            for place in range(away):
                brow = lax.rem((col + 1) * per_share + place, row_blocks)
                rows = pl.ds(pl.multiple_of(brow * width, width), width)
                numer = w_v[rows, :].astype(jnp.float32) * nw[rows, :]
                encode(numer, wq.at[place], wq_scale.at[place])
                w_numer_copy(place).start()
                w_scale_copy(place).start()
            each(n_col, lambda k: h_sum_copy(k).start(), 1)

        when(last, send_w)
        when(i > 1, lambda: send_numer(i - 1))
        nh[i] = jnp.dot(wt_v[...], ratios[...], preferred_element_type=jnp.float32)
        swap(i).start()

        def between():
            receive(1)
            add_w_sums()
            h_out[mine, :] = add_pair(0)

        when(first, between)

    if n_row > UNROLL:
        nw[...] = jnp.zeros_like(nw)
        hsum[...] = jnp.zeros_like(hsum)
    each(n_row, turn)
    send_numer(n_row - 1)
    own = pl.ds(pl.multiple_of(col * share, share), share)
    w_out[...] = w_v[own, :].astype(jnp.float32) * nw[own, :]

    def add_h_numer(i):
        h_numer_arrival(i).wait_recv()
        h_scale_arrival(i).wait_recv()
        h_out[mine, :] = h_out[mine, :] + decode(hq_in[target(i)], hq_scale_in[target(i)])

    each(n_row, add_h_numer, 1)
    h_finish = pltpu.make_async_remote_copy(
        src_ref=h_out.at[mine], dst_ref=h_out.at[mine], send_sem=os_sem, recv_sem=or_sem,
        device_id={"sub": other}, device_id_type=MESH,
    )
    h_finish.start()

    each(n_col, lambda j: h_sum_copy(j).wait(), 1)
    h_total = hsum[0:1, :]
    for j in range(1, n_col):
        h_total = h_total + hrecv[j, 0:1, :]
    for i in range(away):
        rows = pl.ds(i % per_share * width, width)
        w_numer_copy(i).wait()
        w_scale_copy(i).wait()
        total = w_out[rows, :] + decode(wq_in[i], wq_scale_in[i])
        w_out[rows, :] = total / h_total if i >= away - per_share else total

    def settle(j):
        h_copy(j).wait_send()
        h_numer_copy(j).wait_send()
        h_scale_copy(j).wait_send()
        forward(j, mine).wait_send()

    each(n_row, settle, 1)
    h_finish.wait_send()
    h_arrived = pltpu.make_async_remote_copy(
        src_ref=h_out.at[mine], dst_ref=h_out.at[theirs], send_sem=os_sem, recv_sem=or_sem,
        device_id={"sub": other}, device_id_type=MESH,
    )
    h_arrived.wait_recv()


def body(a_blocks, block_list, block_count, w_factor, h_factor):
    n_row, n_col, n_sub = (lax.axis_size(axis) for axis in ("row", "col", "sub"))
    a, lists, counts, w = a_blocks[0, 0], block_list[0, 0], block_count[0, 0], w_factor[0]
    tile_rows, rank = w.shape
    width = h_factor.shape[1]
    half = rank // n_sub
    share = tile_rows // n_col
    away = (tile_rows - share) // width
    f32, bf16, i16, i32 = jnp.float32, jnp.bfloat16, jnp.int16, jnp.int32
    dma = pltpu.SemaphoreType.DMA
    vmem, smem = pltpu.VMEM, pltpu.SMEM
    lists = lists.T
    w_new, h_new = pl.pallas_call(
        functools.partial(kernel, (n_row, n_col, n_sub)),
        out_shape=(
            jax.ShapeDtypeStruct((share, rank), f32),
            jax.ShapeDtypeStruct((rank, width), f32),
        ),
        in_specs=[pl.BlockSpec(memory_space=pltpu.HBM)] * 5,
        out_specs=(pl.BlockSpec(memory_space=vmem), pl.BlockSpec(memory_space=vmem)),
        scratch_shapes=[
            smem(lists.shape, i32),
            smem(counts.shape, i32),
            vmem(a.shape, bf16),
            vmem(w.shape, bf16),
            vmem((rank, tile_rows), bf16),
            vmem((n_row, rank, width), bf16),
            vmem((tile_rows, width), bf16),
            vmem((tile_rows, rank), f32),
            vmem((n_row, rank, width), f32),
            vmem((n_row, half, width), f32),
            vmem((n_row, half, width), i16),
            vmem((n_row, 8, width), f32),
            vmem((n_row, half, width), i16),
            vmem((n_row, 8, width), f32),
            vmem((away, width, rank), i16),
            vmem((away, 8, rank), f32),
            vmem((away, width, rank), i16),
            vmem((away, 8, rank), f32),
            vmem((8, rank), f32),
            vmem((n_col, 8, rank), f32),
            vmem((8, rank), f32),
            vmem((n_row * n_sub, 8, rank), f32),
            vmem((half, width), f32),
            dma((5,)),
            *[dma((n_row,))] * 10,
            *[dma((away,))] * 4,
            *[dma((n_col,))] * 2,
            *[dma((n_row * n_sub,))] * 2,
            dma,
            dma,
        ],
        compiler_params=pltpu.CompilerParams(
            collective_id=0, has_side_effects=True, vmem_limit_bytes=63 * 2**20
        ),
    )(a, lists, counts, w, h_factor)
    return w_new[None], h_new


def solution(mesh):
    placed = (
        P(("grp", "row", "sub"), "col", None, None, None, None),
        P(("grp", "row", "sub"), "col", None, None),
        P(("grp", "row", "sub"), "col", None),
        P(("grp", "row", "sub"), None, None),
        P(None, ("grp", "row", "col")),
    )
    return jax.shard_map(
        body,
        mesh=mesh,
        in_specs=placed,
        out_specs=(P(("grp", "row", "sub"), "col", None), P(None, ("grp", "row", "col"))),
        check_vma=False,
    )
```

```python
import functools
import jax
import jax.numpy as jnp
from jax import lax
from jax.experimental import pallas as pl
from jax.experimental.pallas import tpu as pltpu
from jax.sharding import PartitionSpec as P

MESH = pl.DeviceIdType.MESH
UNROLL = 2
LEVELS = 65535.0
OFFSET = 32768


def when(condition, action):
    if isinstance(condition, bool):
        if condition:
            action()
    else:
        pl.when(condition)(action)


def each(count, action, first=0):
    if count <= UNROLL:
        for i in range(first, count):
            action(i)
    else:

        def step(i, carry):
            action(i)
            return carry

        lax.fori_loop(first, count, step, 0)


def encode(values, code, scale):
    top = jnp.maximum(jnp.max(values, axis=0, keepdims=True), 1e-30)
    steps = (values * (LEVELS / top) + 0.5).astype(jnp.int32) - OFFSET
    code[...] = steps.astype(jnp.int16)
    scale[...] = jnp.broadcast_to(top * (1.0 / LEVELS), scale.shape)


def decode(code, scale):
    return (code.astype(jnp.int32) + OFFSET).astype(jnp.float32) * scale[0:1, :]


def kernel(
    sizes, a_hbm, lists_hbm, counts_hbm, w_hbm, h_hbm, w_out, h_out,
    lists, counts, a_v, w_v, wt_v, hall, ratios, nw, nh, nhx,
    hq, hq_scale, hq_in, hq_scale_in, wq, wq_scale, wq_in, wq_scale_in,
    hsum, hrecv, wsum, wsrecv, w_inverse, load_sem,
    hs_sem, hr_sem, fs_sem, fr_sem, xs_sem, xr_sem, zs_sem, zr_sem, ys_sem, yr_sem,
    ws_sem, wr_sem, vs_sem, vr_sem, gs_sem, gr_sem, ts_sem, tr_sem, os_sem, or_sem,
):
    n_row, n_col, n_sub = sizes
    row, col, sub = lax.axis_index("row"), lax.axis_index("col"), lax.axis_index("sub")
    other = 1 - sub
    row_blocks, slots, width, _ = a_v.shape
    tile_rows, rank = w_v.shape
    half = rank // n_sub
    share = tile_rows // n_col
    per_share = share // width
    away = row_blocks - per_share
    mine = pl.ds(pl.multiple_of(sub * half, half), half)
    theirs = pl.ds(pl.multiple_of(other * half, half), half)

    def ahead(j):
        return lax.rem(row + j, n_row)

    near = jnp.minimum(row, n_row - 1 - row)
    away_side = jnp.where(2 * row < n_row, 1, -1)

    def target(i):
        step = (i + 1) // 2
        sign = 1 - 2 * (i % 2)
        return row + jnp.where(i <= 2 * near, sign * step, away_side * (i - near))

    load_h = pltpu.make_async_copy(h_hbm, hall.at[row], load_sem.at[0])
    load_w = pltpu.make_async_copy(w_hbm, w_v, load_sem.at[1])
    load_a = pltpu.make_async_copy(a_hbm, a_v, load_sem.at[2])
    load_lists = pltpu.make_async_copy(lists_hbm, lists, load_sem.at[3])
    load_counts = pltpu.make_async_copy(counts_hbm, counts, load_sem.at[4])
    load_w.start()
    load_h.start()
    load_lists.start()
    load_counts.start()
    load_a.start()

    barrier = pltpu.get_barrier_semaphore()

    def greet(i):
        jr, js = i // n_sub, i % n_sub
        pl.semaphore_signal(
            barrier, inc=1, device_id={"row": ahead(jr), "sub": lax.rem(sub + js, n_sub)},
            device_id_type=MESH,
        )

    each(n_row * n_sub, greet, 1)

    def greet_col(j):
        pl.semaphore_signal(
            barrier, inc=1, device_id={"col": lax.rem(col + j, n_col)}, device_id_type=MESH
        )

    each(n_col, greet_col, 1)
    pl.semaphore_wait(barrier, n_row * n_sub - 1 + n_col - 1)

    def h_copy(i):
        return pltpu.make_async_remote_copy(
            src_ref=h_hbm.at[mine], dst_ref=hall.at[row, mine],
            send_sem=hs_sem.at[i], recv_sem=hr_sem.at[row],
            device_id={"row": target(i)}, device_id_type=MESH,
        )

    def h_arrival(i):
        return pltpu.make_async_remote_copy(
            src_ref=h_hbm.at[mine], dst_ref=hall.at[target(i), mine],
            send_sem=hs_sem.at[i], recv_sem=hr_sem.at[target(i)],
            device_id={"row": target(i)}, device_id_type=MESH,
        )

    def forward(i, part):
        return pltpu.make_async_remote_copy(
            src_ref=hall.at[target(i), part], dst_ref=hall.at[target(i), part],
            send_sem=fs_sem.at[i], recv_sem=fr_sem.at[i],
            device_id={"sub": other}, device_id_type=MESH,
        )

    def w_sum_copy(i):
        jr, js = i // n_sub, i % n_sub
        return pltpu.make_async_remote_copy(
            src_ref=wsum, dst_ref=wsrecv.at[i],
            send_sem=ts_sem.at[i], recv_sem=tr_sem.at[i],
            device_id={"row": ahead(jr), "sub": lax.rem(sub + js, n_sub)}, device_id_type=MESH,
        )

    def swap(j):
        return pltpu.make_async_remote_copy(
            src_ref=nh.at[j, theirs], dst_ref=nhx.at[j],
            send_sem=xs_sem.at[j], recv_sem=xr_sem.at[j],
            device_id={"sub": other}, device_id_type=MESH,
        )

    def h_numer_copy(i):
        return pltpu.make_async_remote_copy(
            src_ref=hq.at[i], dst_ref=hq_in.at[row],
            send_sem=zs_sem.at[i], recv_sem=zr_sem.at[row],
            device_id={"row": target(i)}, device_id_type=MESH,
        )

    def h_scale_copy(i):
        return pltpu.make_async_remote_copy(
            src_ref=hq_scale.at[i], dst_ref=hq_scale_in.at[row],
            send_sem=ys_sem.at[i], recv_sem=yr_sem.at[row],
            device_id={"row": target(i)}, device_id_type=MESH,
        )

    def h_numer_arrival(i):
        return pltpu.make_async_remote_copy(
            src_ref=hq.at[i], dst_ref=hq_in.at[target(i)],
            send_sem=zs_sem.at[i], recv_sem=zr_sem.at[target(i)],
            device_id={"row": target(i)}, device_id_type=MESH,
        )

    def h_scale_arrival(i):
        return pltpu.make_async_remote_copy(
            src_ref=hq_scale.at[i], dst_ref=hq_scale_in.at[target(i)],
            send_sem=ys_sem.at[i], recv_sem=yr_sem.at[target(i)],
            device_id={"row": target(i)}, device_id_type=MESH,
        )

    def w_numer_copy(i):
        return pltpu.make_async_remote_copy(
            src_ref=wq.at[i], dst_ref=wq_in.at[i],
            send_sem=ws_sem.at[i], recv_sem=wr_sem.at[i],
            device_id={"col": lax.rem(col + 1 + i // per_share, n_col)}, device_id_type=MESH,
        )

    def w_scale_copy(i):
        return pltpu.make_async_remote_copy(
            src_ref=wq_scale.at[i], dst_ref=wq_scale_in.at[i],
            send_sem=vs_sem.at[i], recv_sem=vr_sem.at[i],
            device_id={"col": lax.rem(col + 1 + i // per_share, n_col)}, device_id_type=MESH,
        )

    def h_sum_copy(j):
        return pltpu.make_async_remote_copy(
            src_ref=hsum, dst_ref=hrecv.at[j],
            send_sem=gs_sem.at[j], recv_sem=gr_sem.at[j],
            device_id={"col": lax.rem(col + j, n_col)}, device_id_type=MESH,
        )

    each(n_row, lambda i: h_copy(i).start(), 1)

    load_w.wait()
    wsum[...] = jnp.dot(
        jnp.ones((8, tile_rows), jnp.bfloat16), w_v[...], preferred_element_type=jnp.float32
    )
    each(n_row * n_sub, lambda i: w_sum_copy(i).start(), 1)
    wt_v[...] = w_v[...].T
    load_h.wait()
    load_a.wait()

    load_lists.wait()
    load_counts.wait()

    def add_w_sums():
        def add(i):
            w_sum_copy(i).wait()
            wsrecv[0] = wsrecv[0] + wsrecv[i]

        wsrecv[0] = wsum[...]
        each(n_row * n_sub, add, 1)
        down = lax.broadcasted_iota(jnp.int32, (half, rank), 0) + sub * half
        along = lax.broadcasted_iota(jnp.int32, (half, rank), 1)
        total = jnp.sum(
            jnp.where(down == along, wsrecv[0, 0:1, :], 0.0), axis=1, keepdims=True
        )
        w_inverse[...] = jnp.broadcast_to(1.0 / total, (half, width))

    def add_pair(j):
        swap(j).wait()
        numer = nhx[j] + nh[j, mine, :]
        return hall[target(j), mine, :].astype(jnp.float32) * numer * w_inverse[...]

    def send_numer(j):
        encode(add_pair(j), hq.at[j], hq_scale.at[j])
        h_numer_copy(j).start()
        h_scale_copy(j).start()

    def receive(i):
        h_arrival(i).wait_recv()
        forward(i, mine).start()

    def turn(i):
        first = i == 0
        last = i == n_row - 1
        when(i > 0, lambda: forward(i, theirs).wait_recv())
        block = target(i)
        h_block = hall[block]
        product = jnp.dot(w_v[...], h_block, preferred_element_type=jnp.float32)
        for brow in range(row_blocks):
            position = jnp.int32(0)
            live = jnp.float32(0)
            for slot in range(slots):
                match = (lists[slot, brow] == block) & (slot < counts[brow])
                position = jnp.where(match, slot, position)
                live = jnp.where(match, jnp.float32(1), live)
            rows = slice(brow * width, (brow + 1) * width)
            entries = a_v[brow, position].astype(jnp.float32) * live
            ratios[rows, :] = (entries / product[rows]).astype(jnp.bfloat16)
        if isinstance(i, int):
            when(0 < i < n_row - 1, lambda: receive(i + 1))
        else:
            when((0 < i) & (i < n_row - 1), lambda: receive(i + 1))
        part_w = lax.dot_general(
            ratios[...], h_block, (((1,), (1,)), ((), ())), preferred_element_type=jnp.float32
        )
        part_h = lax.dot_general(
            jnp.ones((8, width), jnp.bfloat16), h_block, (((1,), (1,)), ((), ())),
            preferred_element_type=jnp.float32,
        )
        if isinstance(i, int) and first:
            nw[...] = part_w
            hsum[...] = part_h
        else:
            nw[...] = nw[...] + part_w
            hsum[...] = hsum[...] + part_h

        def send_w():
            for place in range(away):
                brow = lax.rem((col + 1) * per_share + place, row_blocks)
                rows = pl.ds(pl.multiple_of(brow * width, width), width)
                numer = w_v[rows, :].astype(jnp.float32) * nw[rows, :]
                encode(numer, wq.at[place], wq_scale.at[place])
                w_numer_copy(place).start()
                w_scale_copy(place).start()
            each(n_col, lambda k: h_sum_copy(k).start(), 1)

        when(last, send_w)
        when(i > 1, lambda: send_numer(i - 1))
        nh[i] = jnp.dot(wt_v[...], ratios[...], preferred_element_type=jnp.float32)
        swap(i).start()

        def between():
            receive(1)
            add_w_sums()
            h_out[mine, :] = add_pair(0)

        when(first, between)

    if n_row > UNROLL:
        nw[...] = jnp.zeros_like(nw)
        hsum[...] = jnp.zeros_like(hsum)
    each(n_row, turn)
    send_numer(n_row - 1)
    own = pl.ds(pl.multiple_of(col * share, share), share)
    w_out[...] = w_v[own, :].astype(jnp.float32) * nw[own, :]

    def add_h_numer(i):
        h_numer_arrival(i).wait_recv()
        h_scale_arrival(i).wait_recv()
        h_out[mine, :] = h_out[mine, :] + decode(hq_in[target(i)], hq_scale_in[target(i)])

    each(n_row, add_h_numer, 1)
    h_finish = pltpu.make_async_remote_copy(
        src_ref=h_out.at[mine], dst_ref=h_out.at[mine], send_sem=os_sem, recv_sem=or_sem,
        device_id={"sub": other}, device_id_type=MESH,
    )
    h_finish.start()

    each(n_col, lambda j: h_sum_copy(j).wait(), 1)
    h_total = hsum[0:1, :]
    for j in range(1, n_col):
        h_total = h_total + hrecv[j, 0:1, :]
    for i in range(away):
        rows = pl.ds(i % per_share * width, width)
        w_numer_copy(i).wait()
        w_scale_copy(i).wait()
        total = w_out[rows, :] + decode(wq_in[i], wq_scale_in[i])
        w_out[rows, :] = total / h_total if i >= away - per_share else total

    def settle(j):
        h_copy(j).wait_send()
        h_numer_copy(j).wait_send()
        h_scale_copy(j).wait_send()
        forward(j, mine).wait_send()

    each(n_row, settle, 1)
    h_finish.wait_send()
    h_arrived = pltpu.make_async_remote_copy(
        src_ref=h_out.at[mine], dst_ref=h_out.at[theirs], send_sem=os_sem, recv_sem=or_sem,
        device_id={"sub": other}, device_id_type=MESH,
    )
    h_arrived.wait_recv()


def body(a_blocks, block_list, block_count, w_factor, h_factor):
    n_row, n_col, n_sub = (lax.axis_size(axis) for axis in ("row", "col", "sub"))
    a, lists, counts, w = a_blocks[0, 0], block_list[0, 0], block_count[0, 0], w_factor[0]
    tile_rows, rank = w.shape
    width = h_factor.shape[1]
    half = rank // n_sub
    share = tile_rows // n_col
    away = (tile_rows - share) // width
    f32, bf16, i16, i32 = jnp.float32, jnp.bfloat16, jnp.int16, jnp.int32
    dma = pltpu.SemaphoreType.DMA
    vmem, smem = pltpu.VMEM, pltpu.SMEM
    lists = lists.T
    w_new, h_new = pl.pallas_call(
        functools.partial(kernel, (n_row, n_col, n_sub)),
        out_shape=(
            jax.ShapeDtypeStruct((share, rank), f32),
            jax.ShapeDtypeStruct((rank, width), f32),
        ),
        in_specs=[pl.BlockSpec(memory_space=pltpu.HBM)] * 5,
        out_specs=(pl.BlockSpec(memory_space=vmem), pl.BlockSpec(memory_space=vmem)),
        scratch_shapes=[
            smem(lists.shape, i32),
            smem(counts.shape, i32),
            vmem(a.shape, bf16),
            vmem(w.shape, bf16),
            vmem((rank, tile_rows), bf16),
            vmem((n_row, rank, width), bf16),
            vmem((tile_rows, width), bf16),
            vmem((tile_rows, rank), f32),
            vmem((n_row, rank, width), f32),
            vmem((n_row, half, width), f32),
            vmem((n_row, half, width), i16),
            vmem((n_row, 8, width), f32),
            vmem((n_row, half, width), i16),
            vmem((n_row, 8, width), f32),
            vmem((away, width, rank), i16),
            vmem((away, 8, rank), f32),
            vmem((away, width, rank), i16),
            vmem((away, 8, rank), f32),
            vmem((8, rank), f32),
            vmem((n_col, 8, rank), f32),
            vmem((8, rank), f32),
            vmem((n_row * n_sub, 8, rank), f32),
            vmem((half, width), f32),
            dma((5,)),
            *[dma((n_row,))] * 10,
            *[dma((away,))] * 4,
            *[dma((n_col,))] * 2,
            *[dma((n_row * n_sub,))] * 2,
            dma,
            dma,
        ],
        compiler_params=pltpu.CompilerParams(
            collective_id=0, has_side_effects=True, vmem_limit_bytes=63 * 2**20
        ),
    )(a, lists, counts, w, h_factor)
    return w_new[None], h_new


def solution(mesh):
    placed = (
        P(("grp", "row", "sub"), "col", None, None, None, None),
        P(("grp", "row", "sub"), "col", None, None),
        P(("grp", "row", "sub"), "col", None),
        P(("grp", "row", "sub"), None, None),
        P(None, ("grp", "row", "col")),
    )
    return jax.shard_map(
        body,
        mesh=mesh,
        in_specs=placed,
        out_specs=(P(("grp", "row", "sub"), "col", None), P(None, ("grp", "row", "col"))),
        check_vma=False,
    )
```

```python
import functools
import jax
import jax.numpy as jnp
from jax import lax
from jax.experimental import pallas as pl
from jax.experimental.pallas import tpu as pltpu
from jax.sharding import PartitionSpec as P

MESH = pl.DeviceIdType.MESH
UNROLL = 2
LEVELS = 65535.0
OFFSET = 32768
LIMIT = 63 * 2**20
PIECES = 4


def when(condition, action):
    if isinstance(condition, bool):
        if condition:
            action()
    else:
        pl.when(condition)(action)


def each(count, action, first=0):
    if count <= UNROLL:
        for i in range(first, count):
            action(i)
    else:

        def step(i, carry):
            action(i)
            return carry

        lax.fori_loop(first, count, step, 0)


def encode(values, code, scale):
    top = jnp.maximum(jnp.max(values, axis=0, keepdims=True), 1e-30)
    steps = (values * (LEVELS / top) + 0.5).astype(jnp.int32) - OFFSET
    code[...] = steps.astype(jnp.int16)
    scale[...] = jnp.broadcast_to(top * (1.0 / LEVELS), scale.shape)


def decode(code, scale):
    return (code.astype(jnp.int32) + OFFSET).astype(jnp.float32) * scale[0:1, :]


def kernel(
    sizes, a_hbm, lists_hbm, counts_hbm, w_hbm, h_hbm, w_out, h_out,
    lists, counts, a_v, w_v, wt_v, hall, ratios, nw, nh, nhx,
    hq, hq_scale, hq_in, hq_scale_in, wq, wq_scale, wq_in, wq_scale_in,
    hsum, hrecv, wsum, wsrecv, w_inverse, load_sem,
    hs_sem, hr_sem, fs_sem, fr_sem, xs_sem, xr_sem, zs_sem, zr_sem, ys_sem, yr_sem,
    ws_sem, wr_sem, vs_sem, vr_sem, gs_sem, gr_sem, ts_sem, tr_sem, os_sem, or_sem,
):
    n_row, n_col, n_sub = sizes
    row, col, sub = lax.axis_index("row"), lax.axis_index("col"), lax.axis_index("sub")
    other = 1 - sub
    row_blocks, slots, width, _ = a_v.shape
    tile_rows, rank = w_v.shape
    half = rank // n_sub
    share = tile_rows // n_col
    per_share = share // width
    away = row_blocks - per_share
    mine = pl.ds(pl.multiple_of(sub * half, half), half)
    theirs = pl.ds(pl.multiple_of(other * half, half), half)

    def ahead(j):
        return lax.rem(row + j, n_row)

    near = jnp.minimum(row, n_row - 1 - row)
    away_side = jnp.where(2 * row < n_row, 1, -1)

    def target(i):
        step = (i + 1) // 2
        sign = 1 - 2 * (i % 2)
        return row + jnp.where(i <= 2 * near, sign * step, away_side * (i - near))

    load_h = pltpu.make_async_copy(h_hbm, hall.at[row], load_sem.at[0])
    load_w = pltpu.make_async_copy(w_hbm, w_v, load_sem.at[1])
    load_a = pltpu.make_async_copy(a_hbm, a_v, load_sem.at[2])
    load_lists = pltpu.make_async_copy(lists_hbm, lists, load_sem.at[3])
    load_counts = pltpu.make_async_copy(counts_hbm, counts, load_sem.at[4])
    load_w.start()
    load_h.start()
    load_lists.start()
    load_counts.start()
    load_a.start()

    barrier = pltpu.get_barrier_semaphore()

    def greet(i):
        jr, js = i // n_sub, i % n_sub
        pl.semaphore_signal(
            barrier, inc=1, device_id={"row": ahead(jr), "sub": lax.rem(sub + js, n_sub)},
            device_id_type=MESH,
        )

    each(n_row * n_sub, greet, 1)

    def greet_col(j):
        pl.semaphore_signal(
            barrier, inc=1, device_id={"col": lax.rem(col + j, n_col)}, device_id_type=MESH
        )

    each(n_col, greet_col, 1)
    pl.semaphore_wait(barrier, n_row * n_sub - 1 + n_col - 1)

    def h_copy(i):
        return pltpu.make_async_remote_copy(
            src_ref=h_hbm.at[mine], dst_ref=hall.at[row, mine],
            send_sem=hs_sem.at[i], recv_sem=hr_sem.at[row],
            device_id={"row": target(i)}, device_id_type=MESH,
        )

    def h_arrival(i):
        return pltpu.make_async_remote_copy(
            src_ref=h_hbm.at[mine], dst_ref=hall.at[target(i), mine],
            send_sem=hs_sem.at[i], recv_sem=hr_sem.at[target(i)],
            device_id={"row": target(i)}, device_id_type=MESH,
        )

    def forward(i, part):
        return pltpu.make_async_remote_copy(
            src_ref=hall.at[target(i), part], dst_ref=hall.at[target(i), part],
            send_sem=fs_sem.at[i], recv_sem=fr_sem.at[i],
            device_id={"sub": other}, device_id_type=MESH,
        )

    def w_sum_copy(i):
        jr, js = i // n_sub, i % n_sub
        return pltpu.make_async_remote_copy(
            src_ref=wsum, dst_ref=wsrecv.at[i],
            send_sem=ts_sem.at[i], recv_sem=tr_sem.at[i],
            device_id={"row": ahead(jr), "sub": lax.rem(sub + js, n_sub)}, device_id_type=MESH,
        )

    def swap(j):
        return pltpu.make_async_remote_copy(
            src_ref=nh.at[j, theirs], dst_ref=nhx.at[j],
            send_sem=xs_sem.at[j], recv_sem=xr_sem.at[j],
            device_id={"sub": other}, device_id_type=MESH,
        )

    def h_numer_copy(i):
        return pltpu.make_async_remote_copy(
            src_ref=hq.at[i], dst_ref=hq_in.at[row],
            send_sem=zs_sem.at[i], recv_sem=zr_sem.at[row],
            device_id={"row": target(i)}, device_id_type=MESH,
        )

    def h_scale_copy(i):
        return pltpu.make_async_remote_copy(
            src_ref=hq_scale.at[i], dst_ref=hq_scale_in.at[row],
            send_sem=ys_sem.at[i], recv_sem=yr_sem.at[row],
            device_id={"row": target(i)}, device_id_type=MESH,
        )

    def h_numer_arrival(i):
        return pltpu.make_async_remote_copy(
            src_ref=hq.at[i], dst_ref=hq_in.at[target(i)],
            send_sem=zs_sem.at[i], recv_sem=zr_sem.at[target(i)],
            device_id={"row": target(i)}, device_id_type=MESH,
        )

    def h_scale_arrival(i):
        return pltpu.make_async_remote_copy(
            src_ref=hq_scale.at[i], dst_ref=hq_scale_in.at[target(i)],
            send_sem=ys_sem.at[i], recv_sem=yr_sem.at[target(i)],
            device_id={"row": target(i)}, device_id_type=MESH,
        )

    def w_numer_copy(i):
        return pltpu.make_async_remote_copy(
            src_ref=wq.at[i], dst_ref=wq_in.at[i],
            send_sem=ws_sem.at[i], recv_sem=wr_sem.at[i],
            device_id={"col": lax.rem(col + 1 + i // per_share, n_col)}, device_id_type=MESH,
        )

    def w_scale_copy(i):
        return pltpu.make_async_remote_copy(
            src_ref=wq_scale.at[i], dst_ref=wq_scale_in.at[i],
            send_sem=vs_sem.at[i], recv_sem=vr_sem.at[i],
            device_id={"col": lax.rem(col + 1 + i // per_share, n_col)}, device_id_type=MESH,
        )

    def h_sum_copy(j):
        return pltpu.make_async_remote_copy(
            src_ref=hsum, dst_ref=hrecv.at[j],
            send_sem=gs_sem.at[j], recv_sem=gr_sem.at[j],
            device_id={"col": lax.rem(col + j, n_col)}, device_id_type=MESH,
        )

    each(n_row, lambda i: h_copy(i).start(), 1)

    load_w.wait()
    wsum[...] = jnp.dot(
        jnp.ones((8, tile_rows), jnp.bfloat16), w_v[...], preferred_element_type=jnp.float32
    )
    each(n_row * n_sub, lambda i: w_sum_copy(i).start(), 1)
    wt_v[...] = w_v[...].T
    load_h.wait()
    load_a.wait()

    load_lists.wait()
    load_counts.wait()

    def add_w_sums():
        def add(i):
            w_sum_copy(i).wait()
            wsrecv[0] = wsrecv[0] + wsrecv[i]

        wsrecv[0] = wsum[...]
        each(n_row * n_sub, add, 1)
        down = lax.broadcasted_iota(jnp.int32, (half, rank), 0) + sub * half
        along = lax.broadcasted_iota(jnp.int32, (half, rank), 1)
        total = jnp.sum(
            jnp.where(down == along, wsrecv[0, 0:1, :], 0.0), axis=1, keepdims=True
        )
        w_inverse[...] = jnp.broadcast_to(1.0 / total, (half, width))

    def add_pair(j):
        swap(j).wait()
        numer = nhx[j] + nh[j, mine, :]
        return hall[target(j), mine, :].astype(jnp.float32) * numer * w_inverse[...]

    def send_numer(j):
        encode(add_pair(j), hq.at[j], hq_scale.at[j])
        h_numer_copy(j).start()
        h_scale_copy(j).start()

    def receive(i):
        h_arrival(i).wait_recv()
        forward(i, mine).start()

    def turn(i):
        first = i == 0
        last = i == n_row - 1
        when(i > 0, lambda: forward(i, theirs).wait_recv())
        block = target(i)
        h_block = hall[block]
        product = jnp.dot(w_v[...], h_block, preferred_element_type=jnp.float32)
        for brow in range(row_blocks):
            position = jnp.int32(0)
            live = jnp.float32(0)
            for slot in range(slots):
                match = (lists[slot, brow] == block) & (slot < counts[brow])
                position = jnp.where(match, slot, position)
                live = jnp.where(match, jnp.float32(1), live)
            rows = slice(brow * width, (brow + 1) * width)
            entries = a_v[brow, position].astype(jnp.float32) * live
            ratios[rows, :] = (entries / product[rows]).astype(jnp.bfloat16)
        if isinstance(i, int):
            when(0 < i < n_row - 1, lambda: receive(i + 1))
        else:
            when((0 < i) & (i < n_row - 1), lambda: receive(i + 1))
        part_w = lax.dot_general(
            ratios[...], h_block, (((1,), (1,)), ((), ())), preferred_element_type=jnp.float32
        )
        part_h = lax.dot_general(
            jnp.ones((8, width), jnp.bfloat16), h_block, (((1,), (1,)), ((), ())),
            preferred_element_type=jnp.float32,
        )
        if isinstance(i, int) and first:
            nw[...] = part_w
            hsum[...] = part_h
        else:
            nw[...] = nw[...] + part_w
            hsum[...] = hsum[...] + part_h

        def send_w():
            for place in range(away):
                brow = lax.rem((col + 1) * per_share + place, row_blocks)
                rows = pl.ds(pl.multiple_of(brow * width, width), width)
                numer = w_v[rows, :].astype(jnp.float32) * nw[rows, :]
                encode(numer, wq.at[place], wq_scale.at[place])
                w_numer_copy(place).start()
                w_scale_copy(place).start()
            each(n_col, lambda k: h_sum_copy(k).start(), 1)

        when(last, send_w)
        when(i > 1, lambda: send_numer(i - 1))
        nh[i] = jnp.dot(wt_v[...], ratios[...], preferred_element_type=jnp.float32)
        swap(i).start()

        def between():
            receive(1)
            add_w_sums()
            h_out[mine, :] = add_pair(0)

        when(first, between)

    if n_row > UNROLL:
        nw[...] = jnp.zeros_like(nw)
        hsum[...] = jnp.zeros_like(hsum)
    each(n_row, turn)
    send_numer(n_row - 1)
    own = pl.ds(pl.multiple_of(col * share, share), share)
    w_out[...] = w_v[own, :].astype(jnp.float32) * nw[own, :]

    def add_h_numer(i):
        h_numer_arrival(i).wait_recv()
        h_scale_arrival(i).wait_recv()
        h_out[mine, :] = h_out[mine, :] + decode(hq_in[target(i)], hq_scale_in[target(i)])

    each(n_row, add_h_numer, 1)
    h_finish = pltpu.make_async_remote_copy(
        src_ref=h_out.at[mine], dst_ref=h_out.at[mine], send_sem=os_sem, recv_sem=or_sem,
        device_id={"sub": other}, device_id_type=MESH,
    )
    h_finish.start()

    each(n_col, lambda j: h_sum_copy(j).wait(), 1)
    h_total = hsum[0:1, :]
    for j in range(1, n_col):
        h_total = h_total + hrecv[j, 0:1, :]
    for i in range(away):
        rows = pl.ds(i % per_share * width, width)
        w_numer_copy(i).wait()
        w_scale_copy(i).wait()
        total = w_out[rows, :] + decode(wq_in[i], wq_scale_in[i])
        w_out[rows, :] = total / h_total if i >= away - per_share else total

    def settle(j):
        h_copy(j).wait_send()
        h_numer_copy(j).wait_send()
        h_scale_copy(j).wait_send()
        forward(j, mine).wait_send()

    each(n_row, settle, 1)
    h_finish.wait_send()
    h_arrived = pltpu.make_async_remote_copy(
        src_ref=h_out.at[mine], dst_ref=h_out.at[theirs], send_sem=os_sem, recv_sem=or_sem,
        device_id={"sub": other}, device_id_type=MESH,
    )
    h_arrived.wait_recv()


def place_outputs(w_in, h_in, w_out, h_out, sem):
    copies = []
    for source, to in ((w_in, w_out), (h_in, h_out)):
        rows = source.shape[0] // PIECES
        for piece in range(PIECES):
            part = pl.ds(piece * rows, rows)
            copies.append(
                pltpu.make_async_copy(source.at[part], to.at[part], sem.at[len(copies)])
            )
    for copy in copies:
        copy.start()
    for copy in copies:
        copy.wait()


def body(a_blocks, block_list, block_count, w_factor, h_factor):
    n_row, n_col, n_sub = (lax.axis_size(axis) for axis in ("row", "col", "sub"))
    a, lists, counts, w = a_blocks[0, 0], block_list[0, 0], block_count[0, 0], w_factor[0]
    tile_rows, rank = w.shape
    width = h_factor.shape[1]
    half = rank // n_sub
    share = tile_rows // n_col
    away = (tile_rows - share) // width
    f32, bf16, i16, i32 = jnp.float32, jnp.bfloat16, jnp.int16, jnp.int32
    dma = pltpu.SemaphoreType.DMA
    vmem, smem = pltpu.VMEM, pltpu.SMEM
    lists = lists.T
    w_new, h_new = pl.pallas_call(
        functools.partial(kernel, (n_row, n_col, n_sub)),
        out_shape=(
            jax.ShapeDtypeStruct((share, rank), f32),
            jax.ShapeDtypeStruct((rank, width), f32),
        ),
        in_specs=[pl.BlockSpec(memory_space=pltpu.HBM)] * 5,
        out_specs=(pl.BlockSpec(memory_space=vmem), pl.BlockSpec(memory_space=vmem)),
        scratch_shapes=[
            smem(lists.shape, i32),
            smem(counts.shape, i32),
            vmem(a.shape, bf16),
            vmem(w.shape, bf16),
            vmem((rank, tile_rows), bf16),
            vmem((n_row, rank, width), bf16),
            vmem((tile_rows, width), bf16),
            vmem((tile_rows, rank), f32),
            vmem((n_row, rank, width), f32),
            vmem((n_row, half, width), f32),
            vmem((n_row, half, width), i16),
            vmem((n_row, 8, width), f32),
            vmem((n_row, half, width), i16),
            vmem((n_row, 8, width), f32),
            vmem((away, width, rank), i16),
            vmem((away, 8, rank), f32),
            vmem((away, width, rank), i16),
            vmem((away, 8, rank), f32),
            vmem((8, rank), f32),
            vmem((n_col, 8, rank), f32),
            vmem((8, rank), f32),
            vmem((n_row * n_sub, 8, rank), f32),
            vmem((half, width), f32),
            dma((5,)),
            *[dma((n_row,))] * 10,
            *[dma((away,))] * 4,
            *[dma((n_col,))] * 2,
            *[dma((n_row * n_sub,))] * 2,
            dma,
            dma,
        ],
        compiler_params=pltpu.CompilerParams(
            collective_id=0, has_side_effects=True, vmem_limit_bytes=LIMIT
        ),
    )(a, lists, counts, w, h_factor)
    w_new, h_new = pl.pallas_call(
        place_outputs,
        out_shape=(
            jax.ShapeDtypeStruct(w_new.shape, f32),
            jax.ShapeDtypeStruct(h_new.shape, f32),
        ),
        in_specs=[pl.BlockSpec(memory_space=pl.ANY)] * 2,
        out_specs=(pl.BlockSpec(memory_space=pl.ANY),) * 2,
        scratch_shapes=[dma((2 * PIECES,))],
        compiler_params=pltpu.CompilerParams(vmem_limit_bytes=LIMIT),
    )(w_new, h_new)
    return w_new[None], h_new


def solution(mesh):
    placed = (
        P(("grp", "row", "sub"), "col", None, None, None, None),
        P(("grp", "row", "sub"), "col", None, None),
        P(("grp", "row", "sub"), "col", None),
        P(("grp", "row", "sub"), None, None),
        P(None, ("grp", "row", "col")),
    )
    return jax.shard_map(
        body,
        mesh=mesh,
        in_specs=placed,
        out_specs=(P(("grp", "row", "sub"), "col", None), P(None, ("grp", "row", "col"))),
        check_vma=False,
    )
```

```python
import functools
import jax
import jax.numpy as jnp
from jax import lax
from jax.experimental import pallas as pl
from jax.experimental.pallas import tpu as pltpu
from jax.sharding import PartitionSpec as P

MESH = pl.DeviceIdType.MESH
UNROLL = 2
LEVELS = 65535.0
OFFSET = 32768
LIMIT = 63 * 2**20
PIECES = 4


def when(condition, action):
    if isinstance(condition, bool):
        if condition:
            action()
    else:
        pl.when(condition)(action)


def each(count, action, first=0):
    if count <= UNROLL:
        for i in range(first, count):
            action(i)
    else:

        def step(i, carry):
            action(i)
            return carry

        lax.fori_loop(first, count, step, 0)


def encode(values, code, scale):
    top = jnp.maximum(jnp.max(values, axis=0, keepdims=True), 1e-30)
    steps = (values * (LEVELS / top) + 0.5).astype(jnp.int32) - OFFSET
    code[...] = steps.astype(jnp.int16)
    scale[...] = jnp.broadcast_to(top * (1.0 / LEVELS), scale.shape)


def decode(code, scale):
    return (code.astype(jnp.int32) + OFFSET).astype(jnp.float32) * scale[0:1, :]


def kernel(
    sizes, a_hbm, lists_hbm, counts_hbm, w_hbm, h_hbm, w_out, h_out,
    lists, counts, a_v, w_v, wt_v, hall, ratios, nw, nh, nhx,
    hq, hq_scale, hq_in, hq_scale_in, wq, wq_scale, wq_in, wq_scale_in,
    hsum, hrecv, wsum, wsrecv, w_inverse, load_sem,
    hs_sem, hr_sem, fs_sem, fr_sem, xs_sem, xr_sem, zs_sem, zr_sem, ys_sem, yr_sem,
    ws_sem, wr_sem, vs_sem, vr_sem, gs_sem, gr_sem, ts_sem, tr_sem, os_sem, or_sem,
):
    n_row, n_col, n_sub = sizes
    row, col, sub = lax.axis_index("row"), lax.axis_index("col"), lax.axis_index("sub")
    other = 1 - sub
    row_blocks, slots, width, _ = a_v.shape
    tile_rows, rank = w_v.shape
    half = rank // n_sub
    share = tile_rows // n_col
    per_share = share // width
    away = row_blocks - per_share
    mine = pl.ds(pl.multiple_of(sub * half, half), half)
    theirs = pl.ds(pl.multiple_of(other * half, half), half)

    def ahead(j):
        return lax.rem(row + j, n_row)

    near = jnp.minimum(row, n_row - 1 - row)
    away_side = jnp.where(2 * row < n_row, 1, -1)

    def target(i):
        step = (i + 1) // 2
        sign = 1 - 2 * (i % 2)
        return row + jnp.where(i <= 2 * near, sign * step, away_side * (i - near))

    load_h = pltpu.make_async_copy(h_hbm, hall.at[row], load_sem.at[0])
    load_w = pltpu.make_async_copy(w_hbm, w_v, load_sem.at[1])
    load_a = pltpu.make_async_copy(a_hbm, a_v, load_sem.at[2])
    load_lists = pltpu.make_async_copy(lists_hbm, lists, load_sem.at[3])
    load_counts = pltpu.make_async_copy(counts_hbm, counts, load_sem.at[4])
    load_w.start()
    load_h.start()
    load_lists.start()
    load_counts.start()
    load_a.start()

    barrier = pltpu.get_barrier_semaphore()

    def greet(i):
        jr, js = i // n_sub, i % n_sub
        pl.semaphore_signal(
            barrier, inc=1, device_id={"row": ahead(jr), "sub": lax.rem(sub + js, n_sub)},
            device_id_type=MESH,
        )

    each(n_row * n_sub, greet, 1)

    def greet_col(j):
        pl.semaphore_signal(
            barrier, inc=1, device_id={"col": lax.rem(col + j, n_col)}, device_id_type=MESH
        )

    each(n_col, greet_col, 1)
    pl.semaphore_wait(barrier, n_row * n_sub - 1 + n_col - 1)

    def h_copy(i):
        return pltpu.make_async_remote_copy(
            src_ref=hall.at[row, mine], dst_ref=hall.at[row, mine],
            send_sem=hs_sem.at[i], recv_sem=hr_sem.at[row],
            device_id={"row": target(i)}, device_id_type=MESH,
        )

    def h_arrival(i):
        return pltpu.make_async_remote_copy(
            src_ref=hall.at[row, mine], dst_ref=hall.at[target(i), mine],
            send_sem=hs_sem.at[i], recv_sem=hr_sem.at[target(i)],
            device_id={"row": target(i)}, device_id_type=MESH,
        )

    def forward(i, part):
        return pltpu.make_async_remote_copy(
            src_ref=hall.at[target(i), part], dst_ref=hall.at[target(i), part],
            send_sem=fs_sem.at[i], recv_sem=fr_sem.at[i],
            device_id={"sub": other}, device_id_type=MESH,
        )

    def w_sum_copy(i):
        jr, js = i // n_sub, i % n_sub
        return pltpu.make_async_remote_copy(
            src_ref=wsum, dst_ref=wsrecv.at[i],
            send_sem=ts_sem.at[i], recv_sem=tr_sem.at[i],
            device_id={"row": ahead(jr), "sub": lax.rem(sub + js, n_sub)}, device_id_type=MESH,
        )

    def swap(j):
        return pltpu.make_async_remote_copy(
            src_ref=nh.at[j, theirs], dst_ref=nhx.at[j],
            send_sem=xs_sem.at[j], recv_sem=xr_sem.at[j],
            device_id={"sub": other}, device_id_type=MESH,
        )

    def h_numer_copy(i):
        return pltpu.make_async_remote_copy(
            src_ref=hq.at[i], dst_ref=hq_in.at[row],
            send_sem=zs_sem.at[i], recv_sem=zr_sem.at[row],
            device_id={"row": target(i)}, device_id_type=MESH,
        )

    def h_scale_copy(i):
        return pltpu.make_async_remote_copy(
            src_ref=hq_scale.at[i], dst_ref=hq_scale_in.at[row],
            send_sem=ys_sem.at[i], recv_sem=yr_sem.at[row],
            device_id={"row": target(i)}, device_id_type=MESH,
        )

    def h_numer_arrival(i):
        return pltpu.make_async_remote_copy(
            src_ref=hq.at[i], dst_ref=hq_in.at[target(i)],
            send_sem=zs_sem.at[i], recv_sem=zr_sem.at[target(i)],
            device_id={"row": target(i)}, device_id_type=MESH,
        )

    def h_scale_arrival(i):
        return pltpu.make_async_remote_copy(
            src_ref=hq_scale.at[i], dst_ref=hq_scale_in.at[target(i)],
            send_sem=ys_sem.at[i], recv_sem=yr_sem.at[target(i)],
            device_id={"row": target(i)}, device_id_type=MESH,
        )

    def w_numer_copy(i):
        return pltpu.make_async_remote_copy(
            src_ref=wq.at[i], dst_ref=wq_in.at[i],
            send_sem=ws_sem.at[i], recv_sem=wr_sem.at[i],
            device_id={"col": lax.rem(col + 1 + i // per_share, n_col)}, device_id_type=MESH,
        )

    def w_scale_copy(i):
        return pltpu.make_async_remote_copy(
            src_ref=wq_scale.at[i], dst_ref=wq_scale_in.at[i],
            send_sem=vs_sem.at[i], recv_sem=vr_sem.at[i],
            device_id={"col": lax.rem(col + 1 + i // per_share, n_col)}, device_id_type=MESH,
        )

    def h_sum_copy(j):
        return pltpu.make_async_remote_copy(
            src_ref=hsum, dst_ref=hrecv.at[j],
            send_sem=gs_sem.at[j], recv_sem=gr_sem.at[j],
            device_id={"col": lax.rem(col + j, n_col)}, device_id_type=MESH,
        )

    load_h.wait()
    each(n_row, lambda i: h_copy(i).start(), 1)

    load_w.wait()
    wsum[...] = jnp.dot(
        jnp.ones((8, tile_rows), jnp.bfloat16), w_v[...], preferred_element_type=jnp.float32
    )
    each(n_row * n_sub, lambda i: w_sum_copy(i).start(), 1)
    wt_v[...] = w_v[...].T
    load_a.wait()

    load_lists.wait()
    load_counts.wait()

    def add_w_sums():
        def add(i):
            w_sum_copy(i).wait()
            wsrecv[0] = wsrecv[0] + wsrecv[i]

        wsrecv[0] = wsum[...]
        each(n_row * n_sub, add, 1)
        down = lax.broadcasted_iota(jnp.int32, (half, rank), 0) + sub * half
        along = lax.broadcasted_iota(jnp.int32, (half, rank), 1)
        total = jnp.sum(
            jnp.where(down == along, wsrecv[0, 0:1, :], 0.0), axis=1, keepdims=True
        )
        w_inverse[...] = jnp.broadcast_to(1.0 / total, (half, width))

    def add_pair(j):
        swap(j).wait()
        numer = nhx[j] + nh[j, mine, :]
        return hall[target(j), mine, :].astype(jnp.float32) * numer * w_inverse[...]

    def send_numer(j):
        encode(add_pair(j), hq.at[j], hq_scale.at[j])
        h_numer_copy(j).start()
        h_scale_copy(j).start()

    def receive(i):
        h_arrival(i).wait_recv()
        forward(i, mine).start()

    def turn(i):
        first = i == 0
        last = i == n_row - 1
        when(i > 0, lambda: forward(i, theirs).wait_recv())
        block = target(i)
        h_block = hall[block]
        product = jnp.dot(w_v[...], h_block, preferred_element_type=jnp.float32)
        for brow in range(row_blocks):
            position = jnp.int32(0)
            live = jnp.float32(0)
            for slot in range(slots):
                match = (lists[slot, brow] == block) & (slot < counts[brow])
                position = jnp.where(match, slot, position)
                live = jnp.where(match, jnp.float32(1), live)
            rows = slice(brow * width, (brow + 1) * width)
            entries = a_v[brow, position].astype(jnp.float32) * live
            ratios[rows, :] = (entries / product[rows]).astype(jnp.bfloat16)
        if isinstance(i, int):
            when(0 < i < n_row - 1, lambda: receive(i + 1))
        else:
            when((0 < i) & (i < n_row - 1), lambda: receive(i + 1))
        part_w = lax.dot_general(
            ratios[...], h_block, (((1,), (1,)), ((), ())), preferred_element_type=jnp.float32
        )
        part_h = lax.dot_general(
            jnp.ones((8, width), jnp.bfloat16), h_block, (((1,), (1,)), ((), ())),
            preferred_element_type=jnp.float32,
        )
        if isinstance(i, int) and first:
            nw[...] = part_w
            hsum[...] = part_h
        else:
            nw[...] = nw[...] + part_w
            hsum[...] = hsum[...] + part_h

        def send_w():
            for place in range(away):
                brow = lax.rem((col + 1) * per_share + place, row_blocks)
                rows = pl.ds(pl.multiple_of(brow * width, width), width)
                numer = w_v[rows, :].astype(jnp.float32) * nw[rows, :]
                encode(numer, wq.at[place], wq_scale.at[place])
                w_numer_copy(place).start()
                w_scale_copy(place).start()
            each(n_col, lambda k: h_sum_copy(k).start(), 1)

        when(last, send_w)
        when(i > 1, lambda: send_numer(i - 1))
        nh[i] = jnp.dot(wt_v[...], ratios[...], preferred_element_type=jnp.float32)
        swap(i).start()

        def between():
            receive(1)
            add_w_sums()
            h_out[mine, :] = add_pair(0)

        when(first, between)

    if n_row > UNROLL:
        nw[...] = jnp.zeros_like(nw)
        hsum[...] = jnp.zeros_like(hsum)
    each(n_row, turn)
    send_numer(n_row - 1)
    own = pl.ds(pl.multiple_of(col * share, share), share)
    w_out[...] = w_v[own, :].astype(jnp.float32) * nw[own, :]

    def add_h_numer(i):
        h_numer_arrival(i).wait_recv()
        h_scale_arrival(i).wait_recv()
        h_out[mine, :] = h_out[mine, :] + decode(hq_in[target(i)], hq_scale_in[target(i)])

    each(n_row, add_h_numer, 1)
    h_finish = pltpu.make_async_remote_copy(
        src_ref=h_out.at[mine], dst_ref=h_out.at[mine], send_sem=os_sem, recv_sem=or_sem,
        device_id={"sub": other}, device_id_type=MESH,
    )
    h_finish.start()

    each(n_col, lambda j: h_sum_copy(j).wait(), 1)
    h_total = hsum[0:1, :]
    for j in range(1, n_col):
        h_total = h_total + hrecv[j, 0:1, :]
    for i in range(away):
        rows = pl.ds(i % per_share * width, width)
        w_numer_copy(i).wait()
        w_scale_copy(i).wait()
        total = w_out[rows, :] + decode(wq_in[i], wq_scale_in[i])
        w_out[rows, :] = total / h_total if i >= away - per_share else total

    def settle(j):
        h_copy(j).wait_send()
        h_numer_copy(j).wait_send()
        h_scale_copy(j).wait_send()
        forward(j, mine).wait_send()

    each(n_row, settle, 1)
    h_finish.wait_send()
    h_arrived = pltpu.make_async_remote_copy(
        src_ref=h_out.at[mine], dst_ref=h_out.at[theirs], send_sem=os_sem, recv_sem=or_sem,
        device_id={"sub": other}, device_id_type=MESH,
    )
    h_arrived.wait_recv()


def place_outputs(w_in, h_in, w_out, h_out, w_held, h_held, in_sem, out_sem):
    inward, outward = [], []
    for source, held, to in ((h_in, h_held, h_out), (w_in, w_held, w_out)):
        rows = source.shape[0] // PIECES
        for piece in range(PIECES):
            part = pl.ds(piece * rows, rows)
            n = len(inward)
            inward.append(
                pltpu.make_async_copy(source.at[part], held.at[part], in_sem.at[n])
            )
            outward.append(pltpu.make_async_copy(held.at[part], to.at[part], out_sem.at[n]))
    for copy in inward:
        copy.start()
    for copy, onward in zip(inward, outward):
        copy.wait()
        onward.start()
    for onward in outward:
        onward.wait()


def body(a_blocks, block_list, block_count, w_factor, h_factor):
    n_row, n_col, n_sub = (lax.axis_size(axis) for axis in ("row", "col", "sub"))
    a, lists, counts, w = a_blocks[0, 0], block_list[0, 0], block_count[0, 0], w_factor[0]
    tile_rows, rank = w.shape
    width = h_factor.shape[1]
    half = rank // n_sub
    share = tile_rows // n_col
    away = (tile_rows - share) // width
    f32, bf16, i16, i32 = jnp.float32, jnp.bfloat16, jnp.int16, jnp.int32
    dma = pltpu.SemaphoreType.DMA
    vmem, smem = pltpu.VMEM, pltpu.SMEM
    lists = lists.T
    w_new, h_new = pl.pallas_call(
        functools.partial(kernel, (n_row, n_col, n_sub)),
        out_shape=(
            jax.ShapeDtypeStruct((share, rank), f32),
            jax.ShapeDtypeStruct((rank, width), f32),
        ),
        in_specs=[pl.BlockSpec(memory_space=pltpu.HBM)] * 5,
        out_specs=(pl.BlockSpec(memory_space=vmem), pl.BlockSpec(memory_space=vmem)),
        scratch_shapes=[
            smem(lists.shape, i32),
            smem(counts.shape, i32),
            vmem(a.shape, bf16),
            vmem(w.shape, bf16),
            vmem((rank, tile_rows), bf16),
            vmem((n_row, rank, width), bf16),
            vmem((tile_rows, width), bf16),
            vmem((tile_rows, rank), f32),
            vmem((n_row, rank, width), f32),
            vmem((n_row, half, width), f32),
            vmem((n_row, half, width), i16),
            vmem((n_row, 8, width), f32),
            vmem((n_row, half, width), i16),
            vmem((n_row, 8, width), f32),
            vmem((away, width, rank), i16),
            vmem((away, 8, rank), f32),
            vmem((away, width, rank), i16),
            vmem((away, 8, rank), f32),
            vmem((8, rank), f32),
            vmem((n_col, 8, rank), f32),
            vmem((8, rank), f32),
            vmem((n_row * n_sub, 8, rank), f32),
            vmem((half, width), f32),
            dma((5,)),
            *[dma((n_row,))] * 10,
            *[dma((away,))] * 4,
            *[dma((n_col,))] * 2,
            *[dma((n_row * n_sub,))] * 2,
            dma,
            dma,
        ],
        compiler_params=pltpu.CompilerParams(
            collective_id=0, has_side_effects=True, vmem_limit_bytes=LIMIT
        ),
    )(a, lists, counts, w, h_factor)
    w_new, h_new = pl.pallas_call(
        place_outputs,
        out_shape=(
            jax.ShapeDtypeStruct(w_new.shape, f32),
            jax.ShapeDtypeStruct(h_new.shape, f32),
        ),
        in_specs=[pl.BlockSpec(memory_space=pl.ANY)] * 2,
        out_specs=(pl.BlockSpec(memory_space=pl.ANY),) * 2,
        scratch_shapes=[
            vmem(w_new.shape, f32),
            vmem(h_new.shape, f32),
            dma((2 * PIECES,)),
            dma((2 * PIECES,)),
        ],
        compiler_params=pltpu.CompilerParams(vmem_limit_bytes=LIMIT),
    )(w_new, h_new)
    return w_new[None], h_new


def solution(mesh):
    placed = (
        P(("grp", "row", "sub"), "col", None, None, None, None),
        P(("grp", "row", "sub"), "col", None, None),
        P(("grp", "row", "sub"), "col", None),
        P(("grp", "row", "sub"), None, None),
        P(None, ("grp", "row", "col")),
    )
    return jax.shard_map(
        body,
        mesh=mesh,
        in_specs=placed,
        out_specs=(P(("grp", "row", "sub"), "col", None), P(None, ("grp", "row", "col"))),
        check_vma=False,
    )
```

```python
import functools
import jax
import jax.numpy as jnp
from jax import lax
from jax.experimental import pallas as pl
from jax.experimental.pallas import tpu as pltpu
from jax.sharding import PartitionSpec as P

MESH = pl.DeviceIdType.MESH
UNROLL = 2
LEVELS = 65535.0
OFFSET = 32768
LIMIT = 53 * 2**20
PIECES = 4


def when(condition, action):
    if isinstance(condition, bool):
        if condition:
            action()
    else:
        pl.when(condition)(action)


def each(count, action, first=0):
    if count <= UNROLL:
        for i in range(first, count):
            action(i)
    else:

        def step(i, carry):
            action(i)
            return carry

        lax.fori_loop(first, count, step, 0)


def encode(values, code, scale):
    top = jnp.maximum(jnp.max(values, axis=0, keepdims=True), 1e-30)
    steps = (values * (LEVELS / top) + 0.5).astype(jnp.int32) - OFFSET
    code[...] = steps.astype(jnp.int16)
    scale[...] = jnp.broadcast_to(top * (1.0 / LEVELS), scale.shape)


def decode(code, scale):
    return (code.astype(jnp.int32) + OFFSET).astype(jnp.float32) * scale[0:1, :]


def kernel(
    sizes, a_hbm, lists_hbm, counts_hbm, w_hbm, h_hbm, w_out, h_out,
    lists, counts, a_v, w_v, wt_v, hall, ratios, nw, nh, nhx,
    hq, hq_scale, hq_in, hq_scale_in, wq, wq_scale, wq_in, wq_scale_in,
    hsum, hrecv, wsum, wsrecv, w_inverse, load_sem,
    hs_sem, hr_sem, fs_sem, fr_sem, xs_sem, xr_sem, zs_sem, zr_sem, ys_sem, yr_sem,
    ws_sem, wr_sem, vs_sem, vr_sem, gs_sem, gr_sem, ts_sem, tr_sem, os_sem, or_sem,
):
    n_row, n_col, n_sub = sizes
    row, col, sub = lax.axis_index("row"), lax.axis_index("col"), lax.axis_index("sub")
    other = 1 - sub
    row_blocks, slots, width, _ = a_v.shape
    tile_rows, rank = w_v.shape
    half = rank // n_sub
    share = tile_rows // n_col
    per_share = share // width
    away = row_blocks - per_share
    mine = pl.ds(pl.multiple_of(sub * half, half), half)
    theirs = pl.ds(pl.multiple_of(other * half, half), half)

    def ahead(j):
        return lax.rem(row + j, n_row)

    near = jnp.minimum(row, n_row - 1 - row)
    away_side = jnp.where(2 * row < n_row, 1, -1)

    def target(i):
        step = (i + 1) // 2
        sign = 1 - 2 * (i % 2)
        return row + jnp.where(i <= 2 * near, sign * step, away_side * (i - near))

    load_h = pltpu.make_async_copy(h_hbm, hall.at[row], load_sem.at[0])
    load_w = pltpu.make_async_copy(w_hbm, w_v, load_sem.at[1])
    load_a = pltpu.make_async_copy(a_hbm, a_v, load_sem.at[2])
    load_lists = pltpu.make_async_copy(lists_hbm, lists, load_sem.at[3])
    load_counts = pltpu.make_async_copy(counts_hbm, counts, load_sem.at[4])
    load_w.start()
    load_h.start()
    load_lists.start()
    load_counts.start()
    load_a.start()

    barrier = pltpu.get_barrier_semaphore()

    def greet(i):
        jr, js = i // n_sub, i % n_sub
        pl.semaphore_signal(
            barrier, inc=1, device_id={"row": ahead(jr), "sub": lax.rem(sub + js, n_sub)},
            device_id_type=MESH,
        )

    each(n_row * n_sub, greet, 1)

    def greet_col(j):
        pl.semaphore_signal(
            barrier, inc=1, device_id={"col": lax.rem(col + j, n_col)}, device_id_type=MESH
        )

    each(n_col, greet_col, 1)
    pl.semaphore_wait(barrier, n_row * n_sub - 1 + n_col - 1)

    def h_copy(i):
        return pltpu.make_async_remote_copy(
            src_ref=hall.at[row, mine], dst_ref=hall.at[row, mine],
            send_sem=hs_sem.at[i], recv_sem=hr_sem.at[row],
            device_id={"row": target(i)}, device_id_type=MESH,
        )

    def h_arrival(i):
        return pltpu.make_async_remote_copy(
            src_ref=hall.at[row, mine], dst_ref=hall.at[target(i), mine],
            send_sem=hs_sem.at[i], recv_sem=hr_sem.at[target(i)],
            device_id={"row": target(i)}, device_id_type=MESH,
        )

    def forward(i, part):
        return pltpu.make_async_remote_copy(
            src_ref=hall.at[target(i), part], dst_ref=hall.at[target(i), part],
            send_sem=fs_sem.at[i], recv_sem=fr_sem.at[i],
            device_id={"sub": other}, device_id_type=MESH,
        )

    def w_sum_copy(i):
        jr, js = i // n_sub, i % n_sub
        return pltpu.make_async_remote_copy(
            src_ref=wsum, dst_ref=wsrecv.at[i],
            send_sem=ts_sem.at[i], recv_sem=tr_sem.at[i],
            device_id={"row": ahead(jr), "sub": lax.rem(sub + js, n_sub)}, device_id_type=MESH,
        )

    def swap(j):
        return pltpu.make_async_remote_copy(
            src_ref=nh.at[j, theirs], dst_ref=nhx.at[j],
            send_sem=xs_sem.at[j], recv_sem=xr_sem.at[j],
            device_id={"sub": other}, device_id_type=MESH,
        )

    def h_numer_copy(i):
        return pltpu.make_async_remote_copy(
            src_ref=hq.at[i], dst_ref=hq_in.at[row],
            send_sem=zs_sem.at[i], recv_sem=zr_sem.at[row],
            device_id={"row": target(i)}, device_id_type=MESH,
        )

    def h_scale_copy(i):
        return pltpu.make_async_remote_copy(
            src_ref=hq_scale.at[i], dst_ref=hq_scale_in.at[row],
            send_sem=ys_sem.at[i], recv_sem=yr_sem.at[row],
            device_id={"row": target(i)}, device_id_type=MESH,
        )

    def h_numer_arrival(i):
        return pltpu.make_async_remote_copy(
            src_ref=hq.at[i], dst_ref=hq_in.at[target(i)],
            send_sem=zs_sem.at[i], recv_sem=zr_sem.at[target(i)],
            device_id={"row": target(i)}, device_id_type=MESH,
        )

    def h_scale_arrival(i):
        return pltpu.make_async_remote_copy(
            src_ref=hq_scale.at[i], dst_ref=hq_scale_in.at[target(i)],
            send_sem=ys_sem.at[i], recv_sem=yr_sem.at[target(i)],
            device_id={"row": target(i)}, device_id_type=MESH,
        )

    def w_numer_copy(i):
        return pltpu.make_async_remote_copy(
            src_ref=wq.at[i], dst_ref=wq_in.at[i],
            send_sem=ws_sem.at[i], recv_sem=wr_sem.at[i],
            device_id={"col": lax.rem(col + 1 + i // per_share, n_col)}, device_id_type=MESH,
        )

    def w_scale_copy(i):
        return pltpu.make_async_remote_copy(
            src_ref=wq_scale.at[i], dst_ref=wq_scale_in.at[i],
            send_sem=vs_sem.at[i], recv_sem=vr_sem.at[i],
            device_id={"col": lax.rem(col + 1 + i // per_share, n_col)}, device_id_type=MESH,
        )

    def h_sum_copy(j):
        return pltpu.make_async_remote_copy(
            src_ref=hsum, dst_ref=hrecv.at[j],
            send_sem=gs_sem.at[j], recv_sem=gr_sem.at[j],
            device_id={"col": lax.rem(col + j, n_col)}, device_id_type=MESH,
        )

    load_h.wait()
    each(n_row, lambda i: h_copy(i).start(), 1)

    load_w.wait()
    wsum[...] = jnp.dot(
        jnp.ones((8, tile_rows), jnp.bfloat16), w_v[...], preferred_element_type=jnp.float32
    )
    each(n_row * n_sub, lambda i: w_sum_copy(i).start(), 1)
    wt_v[...] = w_v[...].T
    load_a.wait()

    load_lists.wait()
    load_counts.wait()

    def add_w_sums():
        def add(i):
            w_sum_copy(i).wait()
            wsrecv[0] = wsrecv[0] + wsrecv[i]

        wsrecv[0] = wsum[...]
        each(n_row * n_sub, add, 1)
        down = lax.broadcasted_iota(jnp.int32, (half, rank), 0) + sub * half
        along = lax.broadcasted_iota(jnp.int32, (half, rank), 1)
        total = jnp.sum(
            jnp.where(down == along, wsrecv[0, 0:1, :], 0.0), axis=1, keepdims=True
        )
        w_inverse[...] = jnp.broadcast_to(1.0 / total, (half, width))

    def add_pair(j):
        swap(j).wait()
        numer = nhx[j] + nh[j, mine, :]
        return hall[target(j), mine, :].astype(jnp.float32) * numer * w_inverse[...]

    def send_numer(j):
        encode(add_pair(j), hq.at[j], hq_scale.at[j])
        h_numer_copy(j).start()
        h_scale_copy(j).start()

    def receive(i):
        h_arrival(i).wait_recv()
        forward(i, mine).start()

    def turn(i):
        first = i == 0
        last = i == n_row - 1
        when(i > 0, lambda: forward(i, theirs).wait_recv())
        block = target(i)
        h_block = hall[block]
        product = jnp.dot(w_v[...], h_block, preferred_element_type=jnp.float32)
        for brow in range(row_blocks):
            position = jnp.int32(0)
            live = jnp.float32(0)
            for slot in range(slots):
                match = (lists[slot, brow] == block) & (slot < counts[brow])
                position = jnp.where(match, slot, position)
                live = jnp.where(match, jnp.float32(1), live)
            rows = slice(brow * width, (brow + 1) * width)
            entries = a_v[brow, position].astype(jnp.float32) * live
            ratios[rows, :] = (entries / product[rows]).astype(jnp.bfloat16)
        if isinstance(i, int):
            when(0 < i < n_row - 1, lambda: receive(i + 1))
        else:
            when((0 < i) & (i < n_row - 1), lambda: receive(i + 1))
        part_w = lax.dot_general(
            ratios[...], h_block, (((1,), (1,)), ((), ())), preferred_element_type=jnp.float32
        )
        part_h = lax.dot_general(
            jnp.ones((8, width), jnp.bfloat16), h_block, (((1,), (1,)), ((), ())),
            preferred_element_type=jnp.float32,
        )
        if isinstance(i, int) and first:
            nw[...] = part_w
            hsum[...] = part_h
        else:
            nw[...] = nw[...] + part_w
            hsum[...] = hsum[...] + part_h

        def send_w():
            for place in range(away):
                brow = lax.rem((col + 1) * per_share + place, row_blocks)
                rows = pl.ds(pl.multiple_of(brow * width, width), width)
                numer = w_v[rows, :].astype(jnp.float32) * nw[rows, :]
                encode(numer, wq.at[place], wq_scale.at[place])
                w_numer_copy(place).start()
                w_scale_copy(place).start()
            each(n_col, lambda k: h_sum_copy(k).start(), 1)

        when(last, send_w)
        when(i > 1, lambda: send_numer(i - 1))
        nh[i] = jnp.dot(wt_v[...], ratios[...], preferred_element_type=jnp.float32)
        swap(i).start()

        def between():
            receive(1)
            add_w_sums()
            h_out[mine, :] = add_pair(0)

        when(first, between)

    if n_row > UNROLL:
        nw[...] = jnp.zeros_like(nw)
        hsum[...] = jnp.zeros_like(hsum)
    each(n_row, turn)
    send_numer(n_row - 1)
    own = pl.ds(pl.multiple_of(col * share, share), share)
    w_out[...] = w_v[own, :].astype(jnp.float32) * nw[own, :]

    def add_h_numer(i):
        h_numer_arrival(i).wait_recv()
        h_scale_arrival(i).wait_recv()
        h_out[mine, :] = h_out[mine, :] + decode(hq_in[target(i)], hq_scale_in[target(i)])

    each(n_row, add_h_numer, 1)
    h_finish = pltpu.make_async_remote_copy(
        src_ref=h_out.at[mine], dst_ref=h_out.at[mine], send_sem=os_sem, recv_sem=or_sem,
        device_id={"sub": other}, device_id_type=MESH,
    )
    h_finish.start()

    each(n_col, lambda j: h_sum_copy(j).wait(), 1)
    h_total = hsum[0:1, :]
    for j in range(1, n_col):
        h_total = h_total + hrecv[j, 0:1, :]
    for i in range(away):
        rows = pl.ds(i % per_share * width, width)
        w_numer_copy(i).wait()
        w_scale_copy(i).wait()
        total = w_out[rows, :] + decode(wq_in[i], wq_scale_in[i])
        w_out[rows, :] = total / h_total if i >= away - per_share else total

    def settle(j):
        h_copy(j).wait_send()
        h_numer_copy(j).wait_send()
        h_scale_copy(j).wait_send()
        forward(j, mine).wait_send()

    each(n_row, settle, 1)
    h_finish.wait_send()
    h_arrived = pltpu.make_async_remote_copy(
        src_ref=h_out.at[mine], dst_ref=h_out.at[theirs], send_sem=os_sem, recv_sem=or_sem,
        device_id={"sub": other}, device_id_type=MESH,
    )
    h_arrived.wait_recv()


def place_outputs(w_in, h_in, w_out, h_out, sem):
    copies = []
    for source, to in ((w_in, w_out), (h_in, h_out)):
        rows = source.shape[0] // PIECES
        for piece in range(PIECES):
            part = pl.ds(piece * rows, rows)
            copies.append(
                pltpu.make_async_copy(source.at[part], to.at[part], sem.at[len(copies)])
            )
    for copy in copies:
        copy.start()
    for copy in copies:
        copy.wait()


def body(a_blocks, block_list, block_count, w_factor, h_factor):
    n_row, n_col, n_sub = (lax.axis_size(axis) for axis in ("row", "col", "sub"))
    a, lists, counts, w = a_blocks[0, 0], block_list[0, 0], block_count[0, 0], w_factor[0]
    tile_rows, rank = w.shape
    width = h_factor.shape[1]
    half = rank // n_sub
    share = tile_rows // n_col
    away = (tile_rows - share) // width
    f32, bf16, i16, i32 = jnp.float32, jnp.bfloat16, jnp.int16, jnp.int32
    dma = pltpu.SemaphoreType.DMA
    vmem, smem = pltpu.VMEM, pltpu.SMEM
    lists = lists.T
    w_new, h_new = pl.pallas_call(
        functools.partial(kernel, (n_row, n_col, n_sub)),
        out_shape=(
            jax.ShapeDtypeStruct((share, rank), f32),
            jax.ShapeDtypeStruct((rank, width), f32),
        ),
        in_specs=[pl.BlockSpec(memory_space=pltpu.HBM)] * 5,
        out_specs=(pl.BlockSpec(memory_space=vmem), pl.BlockSpec(memory_space=vmem)),
        scratch_shapes=[
            smem(lists.shape, i32),
            smem(counts.shape, i32),
            vmem(a.shape, bf16),
            vmem(w.shape, bf16),
            vmem((rank, tile_rows), bf16),
            vmem((n_row, rank, width), bf16),
            vmem((tile_rows, width), bf16),
            vmem((tile_rows, rank), f32),
            vmem((n_row, rank, width), f32),
            vmem((n_row, half, width), f32),
            vmem((n_row, half, width), i16),
            vmem((n_row, 8, width), f32),
            vmem((n_row, half, width), i16),
            vmem((n_row, 8, width), f32),
            vmem((away, width, rank), i16),
            vmem((away, 8, rank), f32),
            vmem((away, width, rank), i16),
            vmem((away, 8, rank), f32),
            vmem((8, rank), f32),
            vmem((n_col, 8, rank), f32),
            vmem((8, rank), f32),
            vmem((n_row * n_sub, 8, rank), f32),
            vmem((half, width), f32),
            dma((5,)),
            *[dma((n_row,))] * 10,
            *[dma((away,))] * 4,
            *[dma((n_col,))] * 2,
            *[dma((n_row * n_sub,))] * 2,
            dma,
            dma,
        ],
        compiler_params=pltpu.CompilerParams(
            collective_id=0, has_side_effects=True, vmem_limit_bytes=LIMIT
        ),
    )(a, lists, counts, w, h_factor)
    w_new, h_new = pl.pallas_call(
        place_outputs,
        out_shape=(
            jax.ShapeDtypeStruct(w_new.shape, f32),
            jax.ShapeDtypeStruct(h_new.shape, f32),
        ),
        in_specs=[pl.BlockSpec(memory_space=pl.ANY)] * 2,
        out_specs=(pl.BlockSpec(memory_space=pl.ANY),) * 2,
        scratch_shapes=[dma((2 * PIECES,))],
        compiler_params=pltpu.CompilerParams(vmem_limit_bytes=LIMIT),
    )(w_new, h_new)
    return w_new[None], h_new


def solution(mesh):
    placed = (
        P(("grp", "row", "sub"), "col", None, None, None, None),
        P(("grp", "row", "sub"), "col", None, None),
        P(("grp", "row", "sub"), "col", None),
        P(("grp", "row", "sub"), None, None),
        P(None, ("grp", "row", "col")),
    )
    return jax.shard_map(
        body,
        mesh=mesh,
        in_specs=placed,
        out_specs=(P(("grp", "row", "sub"), "col", None), P(None, ("grp", "row", "col"))),
        check_vma=False,
    )
```
